256 devices in a mesh: dp: 8 (over z), seq: 32 (over x, y, core).
Axes of the slice: x: 4, y: 4, z: 8, core: 2. Of those that a mesh axis runs over, the one named last changes fastest.
Arguments:
- inputs: bfloat16 [8, 4096, 2048], P('dp', 'seq'), may hold values from -20 to 20
- queries: bfloat16 [8, 4096, 1024], P('dp', 'seq'), may hold values from -0.5 to 0.5
- values: bfloat16 [8, 4096, 1024], P('dp', 'seq'), may hold values from -6 to 6
- out_grad: bfloat16 [8, 4096, 1024], P('dp', 'seq'), may hold values from -0.09375 to 0.09375
- key_weight: bfloat16 [2048, 1024], P(('dp', 'seq')), may hold values from -0.125 to 0.125
- gate_down: bfloat16 [16, 2048], replicated, may hold values from -1 to 1
- gate_up: bfloat16 [16, 1024], replicated, may hold values from -1.5 to 1.5
- gate_bias: float32 [1024], replicated, may hold values from -1 to 14
Outputs:
- input_grad: bfloat16 [8, 4096, 2048], P('dp', 'seq')
- gate_grad: bfloat16 [8, 4096, 1024], P('dp', 'seq')
- key_weight_grad: float32 [2048, 1024], P(('dp', 'seq'))
- down_grad: float32 [16, 2048], replicated
- up_grad: float32 [16, 1024], replicated
The draws below stay inside these ranges and needn't reach their ends.
All inputs are finite; a program needn't handle non-finite values.
Results may differ from the reference program's by a relative error of at most 0.017.
Values may be sent and summed in bfloat16 or wider, within the bound.
No kernel may reach another device: no remote copies, remote signals or barrier semaphores. Data moves between devices by JAX's collectives and lax.ppermute only.
A program may use at most 128 MiB of HBM per device.

```python
import math
import jax
import jax.numpy as jnp
from jax import lax

D = 2048
HEADS = 8
DK = 128
RANK = 16
GROUP = 64
TOK_DEV = 128
HK = 1024
LENGTH = 4096
SEQS = 8


def sweep_direction_flag(key):
    return jax.random.normal(jax.random.fold_in(key, 101), (D,), jnp.float32) / math.sqrt(D)


def draw_inputs(key, part):
    travel_direction = jnp.clip(sweep_direction_flag(key), -0.09, 0.09)
    key = jax.random.fold_in(key, 1)
    base = jnp.clip(jax.random.normal(key, (SEQS, LENGTH, D), jnp.float32), -6.0, 6.0)
    chains = LENGTH // TOK_DEV
    owners = SEQS * chains
    third = TOK_DEV // 3
    offsets = jax.random.randint(jax.random.fold_in(key, 2), (SEQS, chains), 0, third)
    places = jax.lax.broadcasted_iota(jnp.int32, (SEQS, LENGTH), 1)
    seq_ids = jax.lax.broadcasted_iota(jnp.int32, (SEQS, LENGTH), 0)
    local = places % TOK_DEV
    owner = seq_ids * chains + places // TOK_DEV
    turn = local // third
    spread_off = jnp.repeat(offsets, TOK_DEV, axis=1)
    hits = (local % third == spread_off) & (turn < 3)
    moved = jnp.where(turn == 0, 0, jnp.where(turn == 1, 1, owners // 2))
    target = (owner - moved + owners) % owners
    columns = jax.lax.broadcasted_iota(jnp.int32, (D,), 0) // (D // owners)
    block = ((columns[None, None, :] == target[:, :, None]) & hits[:, :, None]).astype(jnp.float32)
    hit_f = hits.astype(jnp.float32)
    return (base + 12.0 * hit_f[:, :, None] * travel_direction + 12.0 * block).astype(jnp.bfloat16)


def draw_gate_down(key, part):
    travel_direction = sweep_direction_flag(key)
    key = jax.random.fold_in(key, 3)
    rest = jax.random.normal(key, (RANK, D), jnp.float32) / math.sqrt(D)
    rest = jnp.clip(rest, -0.9, 0.9)
    return jnp.concatenate([jnp.clip(travel_direction, -0.9, 0.9)[None], rest[1:]], axis=0).astype(jnp.bfloat16)


def draw_gate_up(key, part):
    key = jax.random.fold_in(key, 5)
    first = -jax.random.uniform(jax.random.fold_in(key, 1), (1, HK), jnp.float32, 0.9, 1.3)
    rest = jnp.clip(0.25 * jax.random.normal(jax.random.fold_in(key, 2), (RANK - 1, HK), jnp.float32), -1.4, 1.4)
    return jnp.concatenate([first, rest], axis=0).astype(jnp.bfloat16)


def draw_gate_bias(key, part):
    key = jax.random.fold_in(key, 7)
    pick = jax.random.uniform(jax.random.fold_in(key, 1), (HEADS,), jnp.float32)
    lowest = pick <= jnp.min(pick)
    highest = pick >= jnp.max(pick)
    fast = ((pick < 0.4) | lowest) & ~highest
    level = jax.random.uniform(jax.random.fold_in(key, 2), (HEADS,), jnp.float32, 0.3, 1.4)
    slow = jnp.log(3.1 * LENGTH / (16.0 * level))
    quick = jax.random.uniform(jax.random.fold_in(key, 3), (HEADS,), jnp.float32, -0.5, 1.0)
    base = jnp.where(fast, quick, slow)
    spread = jax.random.uniform(jax.random.fold_in(key, 4), (HEADS, DK), jnp.float32, -0.3, 0.3)
    return (base[:, None] + spread).reshape(HEADS * DK)


def shard_levels(rng, shape, cuts, least, top_value):
    gain, own = 1.0, jax.random.fold_in(rng, 6)
    for axis_at, shards_of in cuts:
        draws = jnp.exp(jax.random.uniform(jax.random.fold_in(own, axis_at), (shards_of,), jnp.float32, least / len(cuts), top_value / len(cuts)))
        gain = gain * jnp.repeat(draws, shape[axis_at] // shards_of).reshape([-1 if axis == axis_at else 1 for axis in range(len(shape))])
    return gain


def bell_draw(own_key, extent, deviation, reach, pieces=(), held_as=jnp.bfloat16):
    loudness = shard_levels(own_key, extent, pieces, -0.22, 0.18) if pieces else 1.0
    entries = jax.random.normal(own_key, extent, jnp.float32) * deviation * loudness
    return jnp.minimum(jnp.maximum(entries, -reach), reach).astype(held_as)


def setup_inputs(seed: int = 0) -> dict:
    streams_of = jax.random.split(jax.random.key(seed), 9)
    inputs = draw_inputs(jax.random.fold_in(streams_of[8], 71), 0)
    queries = bell_draw(streams_of[1], (SEQS, LENGTH, HK), (DK ** -0.5), 0.5, ((0, 8), (1, 32)))
    values = bell_draw(streams_of[2], (SEQS, LENGTH, HK), 1.0, 6.0, ((0, 8), (1, 32)))
    out_grad = bell_draw(streams_of[3], (SEQS, LENGTH, HK), (LENGTH ** -0.5), 0.09375, ((0, 8), (1, 32)))
    key_weight = bell_draw(streams_of[4], (D, HK), D ** -0.5, 0.125, ((0, 256),))
    gate_down = draw_gate_down(jax.random.fold_in(streams_of[8], 71), 0)
    gate_up = draw_gate_up(jax.random.fold_in(streams_of[8], 71), 0)
    gate_bias = draw_gate_bias(jax.random.fold_in(streams_of[8], 71), 0)
    return {"inputs": inputs, "queries": queries, "values": values, "out_grad": out_grad, "key_weight": key_weight, "gate_down": gate_down, "gate_up": gate_up, "gate_bias": gate_bias}


PRECISION_LEVEL = lax.Precision.HIGHEST


def lower_table():
    rows = lax.broadcasted_iota(jnp.int32, (GROUP, GROUP), 0)
    cols = lax.broadcasted_iota(jnp.int32, (GROUP, GROUP), 1)
    return (rows >= cols).astype(jnp.float32)


def group_deltas(queries, keys, values, out_grad, gamma):
    blocks = queries.shape[0] // GROUP
    shape = (blocks, GROUP, HEADS, DK)
    query_f = queries.reshape(shape).astype(jnp.float32)
    key_f = keys.reshape(shape).astype(jnp.float32)
    value_f = values.reshape(shape).astype(jnp.float32)
    grad_f = out_grad.reshape(shape).astype(jnp.float32)
    lower = lower_table()
    beta = jnp.einsum('ij,njhk->nihk', lower, gamma.reshape(shape), precision=PRECISION_LEVEL)
    span = beta[:, -1]
    query_scaled = query_f * jnp.exp(beta)
    key_scaled = key_f * jnp.exp(-beta)
    key_tail = key_f * jnp.exp(span[:, None] - beta)
    zeros = jnp.zeros((HEADS, DK, DK), jnp.float32)

    def forward(carried_state, item):
        tail_rows, value_rows, step_index = item
        next_piece = jnp.exp(step_index)[..., None] * carried_state + jnp.einsum('qex,qen->exn', tail_rows, value_rows, precision=PRECISION_LEVEL)
        return next_piece, carried_state

    _, states = lax.scan(forward, zeros, (key_tail, value_f, span))

    def backward(gradient_term, item):
        scaled_rows, output_gradient, step_index = item
        current_piece = jnp.exp(step_index)[..., None] * gradient_term + jnp.einsum('qex,qen->exn', scaled_rows, output_gradient, precision=PRECISION_LEVEL)
        return current_piece, gradient_term

    _, grads = lax.scan(backward, zeros, (query_scaled, grad_f, span), reverse=True)
    pairs = jnp.einsum('nihv,njhv->nhij', grad_f, value_f, precision=PRECISION_LEVEL) * lower[None, None]
    query_delta = jnp.exp(beta) * (jnp.einsum('nhkv,nihv->nihk', states, grad_f, precision=PRECISION_LEVEL)
                                   + jnp.einsum('nhij,njhk->nihk', pairs, key_scaled, precision=PRECISION_LEVEL))
    key_delta = (jnp.exp(span[:, None] - beta) * jnp.einsum('nhkv,njhv->njhk', grads, value_f, precision=PRECISION_LEVEL)
                 + jnp.exp(-beta) * jnp.einsum('nhij,nihk->njhk', pairs, query_scaled, precision=PRECISION_LEVEL))
    gate_delta = query_f * query_delta - key_f * key_delta
    total = queries.shape[0]
    return key_delta.reshape(total, HEADS * DK), gate_delta.reshape(total, HEADS * DK)


def one_sequence(item, key_weight, gate_down, gate_up, gate_bias):
    tokens, queries, values, out_grad = item
    keys = jnp.dot(tokens, key_weight, preferred_element_type=jnp.float32).astype(jnp.bfloat16)
    latent = lax.dot_general(tokens, gate_down, (((1,), (1,)), ((), ())), preferred_element_type=jnp.float32).astype(jnp.bfloat16)
    logits = jnp.dot(latent, gate_up, preferred_element_type=jnp.float32) + gate_bias
    gamma = jax.nn.log_sigmoid(logits) / 16.0
    key_delta, gate_delta = group_deltas(queries, keys, values, out_grad, gamma)
    suffix = jnp.cumsum(gate_delta[::-1], axis=0)[::-1]
    gate_grad = (suffix * jax.nn.sigmoid(-logits) / 16.0).astype(jnp.bfloat16)
    key_bf = key_delta.astype(jnp.bfloat16)
    weight_part = lax.dot_general(tokens, key_bf, (((0,), (0,)), ((), ())), preferred_element_type=jnp.float32)
    up_part = lax.dot_general(latent, gate_grad, (((0,), (0,)), ((), ())), preferred_element_type=jnp.float32)
    latent_delta = lax.dot_general(gate_grad, gate_up, (((1,), (1,)), ((), ())), preferred_element_type=jnp.float32).astype(jnp.bfloat16)
    down_part = lax.dot_general(latent_delta, tokens, (((0,), (0,)), ((), ())), preferred_element_type=jnp.float32)
    through_keys = lax.dot_general(key_bf, key_weight, (((1,), (1,)), ((), ())), preferred_element_type=jnp.float32)
    through_gate = jnp.dot(latent_delta, gate_down, preferred_element_type=jnp.float32)
    input_grad = (through_keys + through_gate).astype(jnp.bfloat16)
    return input_grad, gate_grad, weight_part, down_part, up_part


def reference(inputs, queries, values, out_grad, key_weight, gate_down, gate_up, gate_bias):
    def per_sequence(item):
        return one_sequence(item, key_weight, gate_down, gate_up, gate_bias)

    input_grad, gate_grad, weight_parts, down_parts, up_parts = lax.map(per_sequence, (inputs, queries, values, out_grad))
    return (input_grad, gate_grad, jnp.sum(weight_parts, axis=0), jnp.sum(down_parts, axis=0), jnp.sum(up_parts, axis=0))
```

```python
import jax
import jax.numpy as jnp
from jax import lax
from jax.sharding import Mesh, PartitionSpec as P

HEADS = 8
DK = 128
GROUP = 64
HALF = HEADS // 2
WIDTH = HALF * DK
HI = lax.Precision.HIGHEST
F32 = jnp.float32
BF16 = jnp.bfloat16
XY = ("x", "y")
SWAP = ((0, 1), (1, 0))


def swap(a):
    return lax.ppermute(a, "c", SWAP)


def spread(a, axis, count):
    return lax.all_to_all(jnp.broadcast_to(a[None], (count,) + a.shape), axis, 0, 0)


def local(inputs, queries, values, out_grad, key_weight, gate_down, gate_up, gate_bias):
    core = lax.axis_index("c")
    first = core == 0
    zs, ps = lax.axis_size("z"), lax.axis_size("x") * lax.axis_size("y")
    own = inputs[0]
    count, model = own.shape
    rows_w = key_weight.shape[0]
    blocks = 2 * count // GROUP

    def halves(a):
        lo, hi = a[..., :WIDTH], a[..., WIDTH:]
        return jnp.where(first, lo, hi), jnp.where(first, hi, lo)

    def paired(mine, theirs, axis):
        return jnp.concatenate(
            [jnp.where(first, mine, theirs), jnp.where(first, theirs, mine)], axis=axis
        )

    w_mine, w_other = halves(key_weight)
    w_chip = paired(w_mine, swap(w_other), 0)
    w_z = spread(w_chip, "z", zs)
    w_all = spread(w_z, XY, ps)
    w_half = jnp.transpose(w_all, (1, 0, 2, 3)).reshape(model, WIDTH)

    tokens = paired(own, swap(own), 0)
    qvg = jnp.stack([queries[0], values[0], out_grad[0]])
    mine, other = halves(qvg)
    qvg = paired(mine, swap(other), 1)
    shape = (blocks, GROUP, HALF, DK)
    query_f, value_f, grad_f = (qvg[i].reshape(shape).astype(F32) for i in range(3))

    latent = lax.dot_general(
        tokens, gate_down, (((1,), (1,)), ((), ())), preferred_element_type=F32
    ).astype(BF16)
    up_half = halves(gate_up)[0]
    logits = jnp.dot(latent, up_half, preferred_element_type=F32) + halves(gate_bias)[0]
    gamma = jax.nn.log_sigmoid(logits) / 16.0
    rows_idx = lax.broadcasted_iota(jnp.int32, (GROUP, GROUP), 0)
    cols_idx = lax.broadcasted_iota(jnp.int32, (GROUP, GROUP), 1)
    lower = (rows_idx >= cols_idx).astype(F32)
    beta = jnp.einsum("ij,njhk->nihk", lower, gamma.reshape(shape), precision=HI)
    span = beta[:, -1]
    total_log = jnp.sum(span, axis=0)
    exp_beta = jnp.exp(beta)
    exp_neg = jnp.exp(-beta)
    exp_tail = jnp.exp(span[:, None] - beta)
    exp_span = jnp.exp(span)
    query_scaled = query_f * exp_beta

    part = HALF * DK // ps
    decays = lax.all_to_all(jnp.exp(total_log).reshape(ps, part), XY, 0, 0)

    def scan_over_chips(state, reverse):
        pieces = lax.all_to_all(state.reshape(ps, part, DK), XY, 0, 0)
        out = [None] * ps
        run = jnp.zeros((part, DK), F32)
        for i in range(ps):
            at = ps - 1 - i if reverse else i
            out[at] = run
            run = decays[at][:, None] * run + pieces[at]
        return lax.all_to_all(jnp.stack(out), XY, 0, 0).reshape(HALF, DK, DK)

    add_g = jnp.einsum("nqex,nqev->nexv", query_scaled, grad_f, precision=HI)
    start_grad = jnp.zeros((HALF, DK, DK), F32)
    for n in reversed(range(blocks)):
        start_grad = exp_span[n][..., None] * start_grad + add_g[n]
    run = scan_over_chips(start_grad, True)
    grads = [None] * blocks
    for n in reversed(range(blocks)):
        grads[n] = run
        run = exp_span[n][..., None] * run + add_g[n]
    grads = jnp.stack(grads)

    keys = jnp.dot(tokens, w_half, preferred_element_type=F32).astype(BF16)
    key_f = keys.reshape(shape).astype(F32)
    add_s = jnp.einsum("nqex,nqev->nexv", key_f * exp_tail, value_f, precision=HI)
    end_state = jnp.zeros((HALF, DK, DK), F32)
    for n in range(blocks):
        end_state = exp_span[n][..., None] * end_state + add_s[n]
    run = scan_over_chips(end_state, False)
    states = [run]
    for n in range(blocks):
        run = exp_span[n][..., None] * run + add_s[n]
        states.append(run)
    states = jnp.stack(states)

    pairs = jnp.einsum("nihv,njhv->nhij", grad_f, value_f, precision=HI) * lower[None, None]
    key_delta = exp_tail * jnp.einsum(
        "nhkv,njhv->njhk", grads, value_f, precision=HI
    ) + exp_neg * jnp.einsum("nhij,nihk->njhk", pairs, query_scaled, precision=HI)
    key_bf = key_delta.reshape(2 * count, WIDTH).astype(BF16)

    weight_part = lax.dot_general(
        tokens, key_bf, (((0,), (0,)), ((), ())), preferred_element_type=F32
    ).astype(BF16)
    weight_part = weight_part.reshape(zs, ps, 2 * rows_w, WIDTH).transpose(1, 0, 2, 3)
    weight_xy = jnp.sum(lax.all_to_all(weight_part, XY, 0, 0).astype(F32), axis=0)
    weight_z = jnp.sum(
        lax.all_to_all(weight_xy.astype(BF16), "z", 0, 0).astype(F32), axis=0
    )
    w_lo, w_hi = weight_z[:rows_w], weight_z[rows_w:]
    key_weight_grad = paired(
        jnp.where(first, w_lo, w_hi), swap(jnp.where(first, w_hi, w_lo)), 1
    )

    query_delta = exp_beta * (
        jnp.einsum("nhkv,nihv->nihk", states[:-1], grad_f, precision=HI)
        + jnp.einsum("nhij,njhk->nihk", pairs, key_f * exp_neg, precision=HI)
    )
    gate_delta = query_f * query_delta - key_f * key_delta
    within = jnp.einsum("ij,njhk->nihk", lower.T, gate_delta, precision=HI)
    beyond = jnp.sum(states[1:] * grads, axis=-1)
    suffix = within + beyond[:, None]
    gate_half = (suffix.reshape(2 * count, WIDTH) * jax.nn.sigmoid(-logits) / 16.0).astype(BF16)
    gate_lo, gate_hi = gate_half[:count], gate_half[count:]
    gate_grad = paired(
        jnp.where(first, gate_lo, gate_hi), swap(jnp.where(first, gate_hi, gate_lo)), 1
    )

    up_part = lax.dot_general(
        latent, gate_half, (((0,), (0,)), ((), ())), preferred_element_type=F32
    )
    latent_part = lax.dot_general(
        gate_half, up_half, (((1,), (1,)), ((), ())), preferred_element_type=F32
    )
    latent_delta = (latent_part + swap(latent_part)).astype(BF16)
    tokens_half = jnp.where(first, tokens[:, : model // 2], tokens[:, model // 2 :])
    down_part = lax.dot_general(
        latent_delta, tokens_half, (((0,), (0,)), ((), ())), preferred_element_type=F32
    )
    rank = gate_up.shape[0]
    small = jnp.concatenate([up_part, down_part], axis=1).reshape(ps, -1, DK)
    small = jnp.sum(lax.all_to_all(small, XY, 0, 0), axis=0)
    small = jnp.sum(spread(small, "z", zs), axis=0)
    small = spread(small, XY, ps).reshape(rank, -1)
    small_other = swap(small)
    up_grad = paired(small[:, :WIDTH], small_other[:, :WIDTH], 1)
    down_grad = paired(small[:, WIDTH:], small_other[:, WIDTH:], 1)

    through_keys = lax.dot_general(
        key_bf, w_half, (((1,), (1,)), ((), ())), preferred_element_type=F32
    )
    keys_lo, keys_hi = through_keys[:count], through_keys[count:]
    own_keys = jnp.where(first, keys_lo, keys_hi) + swap(jnp.where(first, keys_hi, keys_lo))
    own_latent = jnp.where(first, latent_delta[:count], latent_delta[count:])
    through_gate = jnp.dot(own_latent, gate_down, preferred_element_type=F32)
    input_grad = (own_keys + through_gate).astype(BF16)
    return (input_grad[None], gate_grad[None], key_weight_grad, down_grad, up_grad)


def solution(mesh):
    grid = Mesh(mesh.devices.reshape(8, 4, 4, 2), ("z", "x", "y", "c"))
    seq = ("x", "y", "c")
    tok = P("z", seq, None)
    row = P(("z",) + seq, None)
    return jax.shard_map(
        local,
        mesh=grid,
        in_specs=(tok, tok, tok, tok, row, P(), P(), P()),
        out_specs=(tok, tok, row, P(), P()),
        check_vma=False,
    )
```

```python
import jax
import jax.numpy as jnp
from jax import lax
from jax.experimental import pallas as pl
from jax.experimental.pallas import tpu as pltpu
from jax.sharding import Mesh, PartitionSpec as P

HEADS = 8
DK = 128
GROUP = 64
HALF = HEADS // 2
WIDTH = HALF * DK
TOK = 128
PAIR = 2 * TOK
BLOCKS = PAIR // GROUP
MODEL = 2048
RANK = 16
ZS = 8
PS = 16
ROWS = HALF * DK // PS
F32 = jnp.float32
BF16 = jnp.bfloat16
XY = ("x", "y")
SWAP = ((0, 1), (1, 0))
MB = 1 << 20


def shape(dims, dtype=F32):
    return jax.ShapeDtypeStruct(dims, dtype)


BIG = 56
KEYS = 16


def kernel(body, outs, name, limit, scratch=(), specs=None):
    extra = {} if specs is None else {"in_specs": specs}
    return pl.pallas_call(
        body,
        out_shape=outs,
        name=name,
        scratch_shapes=scratch,
        compiler_params=pltpu.CompilerParams(vmem_limit_bytes=limit * MB),
        **extra,
    )


def split(a):
    hi = a.astype(BF16)
    return hi, (a - hi.astype(F32)).astype(BF16)


def dot(a, b, dims=((1,), (0,))):
    return lax.dot_general(a, b, (dims, ((), ())), preferred_element_type=F32)


NT = ((1,), (1,))
TN = ((0,), (0,))


def dot_hl(a, b, dims=((1,), (0,))):
    hi, lo = split(b)
    return dot(a, hi, dims) + dot(a, lo, dims)


def dot_ff(a, b, dims=((1,), (0,))):
    ah, al = split(a)
    bh, bl = split(b)
    return dot(ah, bh, dims) + dot(ah, bl, dims) + dot(al, bh, dims)


def dot_mask(mask, b):
    hi, lo = split(b)
    rest = (b - hi.astype(F32) - lo.astype(F32)).astype(BF16)
    return dot(mask, hi) + dot(mask, lo) + dot(mask, rest)


def is_first():
    return lax.axis_index("c") == 0


def pick(first, a, b):
    return jnp.where(first, a, b)


def low_mask():
    rows = lax.broadcasted_iota(jnp.int32, (GROUP, GROUP), 0)
    cols = lax.broadcasted_iota(jnp.int32, (GROUP, GROUP), 1)
    return rows >= cols, rows <= cols


def tok_of(n):
    return slice(n * GROUP, (n + 1) * GROUP)


def col_of(h):
    return slice(h * DK, (h + 1) * DK)


def span_of(beta, n):
    return beta[(n + 1) * GROUP - 1 : (n + 1) * GROUP]


def prep_body(q, g, v, w, give):
    first = is_first()
    for i, ref in enumerate((q, g, v)):
        give[i * TOK : (i + 1) * TOK] = pick(first, ref[:, WIDTH:], ref[:, :WIDTH])
    rows = pick(first, w[:, WIDTH:], w[:, :WIDTH]).astype(F32)
    give[3 * TOK :] = jnp.concatenate([rows, jnp.zeros_like(rows)], axis=0).astype(BF16)


def gates_body(own, peer, down, up, bias, q, g, v, w, got,
               tok, lat, logit, beta, q_o, g_o, v_o, w_o, adds, send):
    first = is_first()
    tok[:TOK] = pick(first, own[...], peer[...])
    tok[TOK:] = pick(first, peer[...], own[...])
    for i, (ref, out) in enumerate(((q, q_o), (g, g_o), (v, v_o))):
        mine = pick(first, ref[:, :WIDTH], ref[:, WIDTH:])
        theirs = got[i * TOK : (i + 1) * TOK]
        out[:TOK] = pick(first, mine, theirs)
        out[TOK:] = pick(first, theirs, mine)
    mine = pick(first, w[:, :WIDTH], w[:, WIDTH:]).astype(F32)
    theirs = got[3 * TOK :].astype(F32)[:8]
    w_o[...] = jnp.concatenate(
        [pick(first, mine, theirs), pick(first, theirs, mine)], axis=0
    ).astype(BF16)
    latent = dot(tok[...], down[...], NT).astype(BF16)
    lat[...] = latent
    up_half = pick(first, up[:, :WIDTH], up[:, WIDTH:])
    bias_half = pick(first, bias[:, :WIDTH], bias[:, WIDTH:])
    x = dot(latent, up_half) + bias_half
    logit[...] = x
    gamma = (jnp.minimum(x, 0.0) - jnp.log1p(jnp.exp(-jnp.abs(x)))) * (1.0 / 16.0)
    lower = low_mask()[0].astype(BF16)
    run = [jnp.zeros((DK, DK), F32)] * HALF
    total = jnp.zeros((1, WIDTH), F32)
    for n in reversed(range(BLOCKS)):
        b = dot_mask(lower, gamma[tok_of(n)])
        beta[tok_of(n)] = b
        last = b[GROUP - 1 : GROUP]
        total = total + last
        decay = jnp.exp(last)
        scaled = q_o[tok_of(n)].astype(F32) * jnp.exp(b)
        grad = g_o[tok_of(n)]
        for h in range(HALF):
            part = dot_hl(grad[:, col_of(h)], scaled[:, col_of(h)], TN)
            adds[n, col_of(h)] = part
            run[h] = decay[:, col_of(h)] * run[h] + part
    decay = jnp.exp(total)
    for p in range(PS):
        h, at = p // PER, (p % PER) * ROWS
        send[p, :ROWS] = run[h][at : at + ROWS]
        send[p, ROWS:] = jnp.broadcast_to(decay[:, col_of(h)], (8, DK))


def scan_back_body(recv, wz, send):
    run = jnp.zeros((ROWS, DK), F32)
    w = wz[...]
    for p in reversed(range(PS)):
        send[p, : ZS * 16] = w
        wide = jnp.concatenate([run[8 * i : 8 * i + 8] for i in range(ROWS // 8)], axis=1)
        hi = wide.astype(BF16).astype(F32)
        send[p, ZS * 16 :] = jnp.concatenate([hi, wide - hi], axis=0).astype(BF16)
        run = recv[p, ROWS : ROWS + 1] * run + recv[p, :ROWS]


def unpack_w(recv, w):
    for p in range(PS):
        for z in range(ZS):
            w[z * 256 + p * 16 : z * 256 + p * 16 + 16] = recv[p, z * 16 : z * 16 + 16]


def added_states(key, v, beta, n):
    b = beta[tok_of(n)]
    last = b[GROUP - 1 : GROUP]
    tail = key[tok_of(n)].astype(F32) * jnp.exp(last - b)
    vals = v[tok_of(n)]
    return [dot_hl(vals[:, col_of(h)], tail[:, col_of(h)], TN) for h in range(HALF)], jnp.exp(last)


def keys_body(recv, tok, beta, v, key_o, send, w):
    unpack_w(recv, w)
    key_o[...] = dot(tok[...], w[...]).astype(BF16)
    run = [jnp.zeros((DK, DK), F32)] * HALF
    for n in range(BLOCKS):
        parts, decay = added_states(key_o, v, beta, n)
        run = [decay[:, col_of(h)] * run[h] + parts[h] for h in range(HALF)]
    for p in range(PS):
        h, at = p // PER, (p % PER) * ROWS
        send[p] = run[h][at : at + ROWS]


def scan_fwd_body(recv, old, after, send):
    run = jnp.zeros((ROWS, DK), F32)
    for p in range(PS):
        send[p] = run
        run = old[p, ROWS : ROWS + 1] * run + recv[p]


def delta_body(q_r, g_r, v_r, key_r, beta, recv, adds, tok,
               kd_o, local, gin, o_0, o_1, o_2, o_3, blocks):
    low, high = low_mask()
    for p in range(PS):
        both = recv[p, ZS * 16 :].astype(F32)
        wide = both[:8] + both[8:]
        for i in range(ROWS // 8):
            gin[p * ROWS + 8 * i : p * ROWS + 8 * i + 8] = wide[:, col_of(i)]
    run = [gin[col_of(h)] for h in range(HALF)]
    for n in reversed(range(BLOCKS)):
        b = beta[tok_of(n)]
        last = b[GROUP - 1 : GROUP]
        grow, shrink, tail = jnp.exp(b), jnp.exp(-b), jnp.exp(last - b)
        decay = jnp.exp(last)
        q = q_r[tok_of(n)].astype(F32)
        k = key_r[tok_of(n)].astype(F32)
        q_s, k_s = q * grow, k * shrink
        for h in range(HALF):
            c = col_of(h)
            g, v = g_r[tok_of(n), c], v_r[tok_of(n), c]
            pairs = jnp.where(low, dot(g, v, NT), 0.0)
            pairs_t = jnp.where(high, dot(v, g, NT), 0.0)
            kd = tail[:, c] * dot_hl(v, run[h]) + shrink[:, c] * dot_ff(pairs_t, q_s[:, c])
            qd = grow[:, c] * dot_ff(pairs, k_s[:, c])
            kd_o[tok_of(n), c] = kd.astype(BF16)
            local[tok_of(n), c] = q[:, c] * qd - k[:, c] * kd
            run[h] = decay[:, c] * run[h] + adds[n, c]
    kd = kd_o[...]
    for z in range(ZS):
        block = dot(tok[:, z * 256 : z * 256 + 256], kd, TN).astype(BF16)
        for x in range(4):
            blocks[x, z] = block[x * 64 : x * 64 + 64]
    place = lax.axis_index("x")
    for k, out in enumerate((o_0, o_1, o_2, o_3)):
        to = lax.rem(place + k, 4)
        for z in range(ZS):
            for y in range(4):
                out[y, z * 16 : z * 16 + 16] = blocks[to, z, y * 16 : y * 16 + 16]


def y_body(a, b, c, d, own, o_1, o_2, o_3, total):
    for y in range(4):
        total[y] = (a[y].astype(F32) + b[y].astype(F32)) + (c[y].astype(F32) + d[y].astype(F32))
    place = lax.axis_index("y")
    own[...] = total[place]
    for k, out in enumerate((o_1, o_2, o_3)):
        out[...] = total[lax.rem(place + k + 1, 4)].astype(BF16)


def gate_body(sin, gin, key_r, v_r, beta, q_r, g_r, local, logit, lat, up,
              gate_o, gate_keep, gate_give, up_part, lat_part, delta):
    first = is_first()
    high = low_mask()[1].astype(BF16)
    run = [sin[h * PER : (h + 1) * PER].reshape(DK, DK) for h in range(HALF)]
    for n in range(BLOCKS):
        parts, decay = added_states(key_r, v_r, beta, n)
        qd = jnp.concatenate(
            [dot_hl(g_r[tok_of(n), col_of(h)], run[h]) for h in range(HALF)], axis=1
        ) * jnp.exp(beta[tok_of(n)])
        delta[tok_of(n)] = q_r[tok_of(n)].astype(F32) * qd + local[tok_of(n)]
        run = [decay[:, col_of(h)] * run[h] + parts[h] for h in range(HALF)]
    beyond = jnp.concatenate(
        [jnp.sum(run[h] * gin[col_of(h)], axis=0, keepdims=True) for h in range(HALF)], axis=1
    )
    for n in reversed(range(BLOCKS)):
        suffix = dot_mask(high, delta[tok_of(n)]) + beyond
        beyond = suffix[:1]
        x = logit[tok_of(n)]
        gate_o[tok_of(n)] = (suffix * (1.0 / (1.0 + jnp.exp(x))) * (1.0 / 16.0)).astype(BF16)
    gate = gate_o[...]
    gate_keep[...] = pick(first, gate[:TOK], gate[TOK:])
    gate_give[...] = pick(first, gate[TOK:], gate[:TOK])
    up_half = pick(first, up[:, :WIDTH], up[:, WIDTH:])
    up_part[...] = dot(lat[...], gate, TN)
    lat_part[...] = dot(gate, up_half, NT)


def down_body(lat_a, lat_b, tok, up_part, lat_o, send):
    first = is_first()
    latent = (lat_a[...] + lat_b[...]).astype(BF16)
    lat_o[...] = pick(first, latent[:TOK], latent[TOK:])
    half = MODEL // 2
    down = dot(latent, pick(first, tok[:, :half], tok[:, half:]), TN)
    for j in range(WIDTH // DK):
        send[:, j] = up_part[:, col_of(j)]
    for j in range(half // DK):
        send[:, WIDTH // DK + j] = down[:, col_of(j)]


def through_body(kd, recv, keep, give, w):
    first = is_first()
    unpack_w(recv, w)
    mine = pick(first, kd[:TOK], kd[TOK:])
    other = pick(first, kd[TOK:], kd[:TOK])
    give[...] = dot(other, w[...], NT)
    keep[...] = dot(mine, w[...], NT)


def input_body(keep, got, lat, down, out):
    out[...] = (keep[...] + got[...] + dot(lat[...], down[...])).astype(BF16)


PARTS = (WIDTH + MODEL // 2) // DK
PER = DK // ROWS


def mid_body(own, a, b, c, small, send):
    wsum = (own[...] + a[...].astype(F32)) + (b[...].astype(F32) + c[...].astype(F32))
    total = jnp.sum(small[...], axis=0)
    wide = jnp.concatenate(
        [jnp.concatenate([total[4 * i + j : 4 * i + j + 1] for j in range(4)], axis=1)
         for i in range(PARTS // 4)], axis=0)
    hi = wide.astype(BF16).astype(F32)
    extra = jnp.concatenate([hi, wide - hi, jnp.zeros((10, WIDTH), F32)], axis=0).astype(BF16)
    for z in range(ZS):
        send[z, :16] = wsum[z * 16 : z * 16 + 16].astype(BF16)
        send[z, 16:] = extra


def last_body(recv, keep, give):
    first = is_first()
    total = jnp.sum(recv[...].astype(F32), axis=0)
    small = total[16:19] + total[19:22]
    pad = jnp.zeros((5, WIDTH), F32)
    keep[...] = jnp.concatenate([pick(first, total[:8], total[8:16]), small, pad], axis=0)
    give[...] = jnp.concatenate([pick(first, total[8:16], total[:8]), small, pad], axis=0)


def pack_body(mine, theirs, w_o, send):
    first = is_first()
    a, b = pick(first, mine[...], theirs[...]), pick(first, theirs[...], mine[...])
    w_o[:, :WIDTH] = a[:8]
    w_o[:, WIDTH:] = b[:8]
    both = jnp.concatenate([a[8:11], b[8:11], jnp.zeros((2, WIDTH), F32)], axis=0)
    for p in range(PS):
        send[p] = both


def out_body(recv, down_o, up_o):
    for half in range(2):
        at = half * 3
        up_o[:, half * WIDTH : (half + 1) * WIDTH] = recv[:, at]
        for i in range(2):
            lo = half * 2 * WIDTH + i * WIDTH
            down_o[:, lo : lo + WIDTH] = recv[:, at + 1 + i]


def swap(a):
    return lax.ppermute(a, "c", SWAP)


def ring(a, axis, step):
    return lax.ppermute(a, axis, [(i, (i + step) % 4) for i in range(4)])


def a2a(a, axis):
    return lax.all_to_all(a, axis, 0, 0)


def local(inputs, queries, values, out_grad, key_weight, gate_down, gate_up, gate_bias):
    first = is_first()
    own = inputs[0]
    q, g, v = queries[0], out_grad[0], values[0]
    give = kernel(prep_body, shape((3 * TOK + 16, WIDTH), BF16), "prep", 8)(q, g, v, key_weight)
    half_bf = shape((PAIR, WIDTH), BF16)
    half_f = shape((PAIR, WIDTH))
    tok, lat, logit, beta, q, g, v, wz, add_g, send1 = kernel(
        gates_body,
        (shape((PAIR, MODEL), BF16), shape((PAIR, RANK), BF16), half_f, half_f,
         half_bf, half_bf, half_bf, shape((16, WIDTH), BF16),
         shape((BLOCKS, WIDTH, DK)), shape((PS, ROWS + 8, DK))),
        "gates", BIG,
    )(own, swap(own), gate_down, gate_up, gate_bias[None], q, g, v, key_weight, swap(give))
    place = lax.axis_index("z")
    for bit in (1, 2, 4):
        other = lax.ppermute(wz, "z", [(i, i ^ bit) for i in range(ZS)])
        even = (place & bit) == 0
        wz = jnp.concatenate([jnp.where(even, wz, other), jnp.where(even, other, wz)], axis=0)

    recv1 = a2a(send1, XY)
    send2 = kernel(scan_back_body, shape((PS, ZS * 16 + 16, WIDTH), BF16), "scan_back", 8)(recv1, wz)
    recv2 = a2a(send2, XY)
    keys, send3 = kernel(
        keys_body, (half_bf, shape((PS, ROWS, DK))), "keys", KEYS,
        scratch=[pltpu.VMEM((MODEL, WIDTH), BF16)],
    )(recv2, tok, beta, v)
    recv3 = a2a(send3, XY)
    kd, local_part, gin, o_0, o_1, o_2, o_3 = kernel(
        delta_body,
        (half_bf, half_f, shape((WIDTH, DK))) + (shape((4, ZS * 16, WIDTH), BF16),) * 4,
        "delta", BIG, scratch=[pltpu.VMEM((4, ZS, 64, WIDTH), BF16)],
    )(q, g, v, keys, beta, recv2, add_g, tok)
    x_sums = [ring(a, "x", k + 1) for k, a in enumerate((o_1, o_2, o_3))]
    send4 = kernel(
        scan_fwd_body, shape((PS, ROWS, DK)), "scan_fwd", 8,
        specs=[pl.BlockSpec(memory_space=pltpu.VMEM)] * 2 + [pl.BlockSpec(memory_space=pl.ANY)],
    )(recv3, recv1, kd)
    recv4 = a2a(send4, XY)
    y_own, y_1, y_2, y_3 = kernel(
        y_body,
        (shape((ZS * 16, WIDTH)),) + (shape((ZS * 16, WIDTH), BF16),) * 3,
        "y_sums", BIG, scratch=[pltpu.VMEM((4, ZS * 16, WIDTH), F32)],
    )(o_0, *x_sums)
    y_sums = [ring(a, "y", k + 1) for k, a in enumerate((y_1, y_2, y_3))]
    gate, gate_m, gate_x, up_part, lat_part = kernel(
        gate_body,
        (half_bf, shape((TOK, WIDTH), BF16), shape((TOK, WIDTH), BF16),
         shape((RANK, WIDTH)), shape((PAIR, RANK))),
        "gate", BIG, scratch=[pltpu.VMEM((PAIR, WIDTH), F32)],
    )(recv4, gin, keys, v, beta, q, g, local_part, logit, lat, gate_up)
    lat_own, send5 = kernel(
        down_body, (shape((TOK, RANK), BF16), shape((PS, PARTS, DK))), "down", 8
    )(lat_part, swap(lat_part), tok, up_part)
    send6 = kernel(mid_body, shape((ZS, 32, WIDTH), BF16), "mid", 8)(
        y_own, *y_sums, a2a(send5, XY)
    )
    recv6 = a2a(send6, "z")
    keep, theirs = kernel(last_body, (shape((16, WIDTH)), shape((16, WIDTH))), "last", 4)(recv6)
    key_weight_grad, send7 = kernel(
        pack_body, (shape((8, 2 * WIDTH)), shape((PS, 8, WIDTH))), "pack", 4
    )(keep, swap(theirs))
    down_grad, up_grad = kernel(
        out_body, (shape((RANK, MODEL)), shape((RANK, 2 * WIDTH))), "grads", 4
    )(a2a(send7, XY))

    gate_p = swap(gate_x)
    gate_grad = jnp.concatenate(
        [jnp.where(first, gate_m, gate_p), jnp.where(first, gate_p, gate_m)], axis=1
    )
    mine, other = kernel(
        through_body, (shape((TOK, MODEL)), shape((TOK, MODEL))), "through", BIG,
        scratch=[pltpu.VMEM((MODEL, WIDTH), BF16)],
    )(kd, recv2)
    input_grad = kernel(input_body, shape((TOK, MODEL), BF16), "input", 16)(
        mine, swap(other), lat_own, gate_down
    )
    return (input_grad[None], gate_grad[None], key_weight_grad, down_grad, up_grad)


def solution(mesh):
    grid = Mesh(mesh.devices.reshape(8, 4, 4, 2), ("z", "x", "y", "c"))
    seq = ("x", "y", "c")
    tok = P("z", seq, None)
    row = P(("z",) + seq, None)
    return jax.shard_map(
        local,
        mesh=grid,
        in_specs=(tok, tok, tok, tok, row, P(), P(), P()),
        out_specs=(tok, tok, row, P(), P()),
        check_vma=False,
    )
```

```python
import jax
import jax.numpy as jnp
from jax import lax
from jax.experimental import pallas as pl
from jax.experimental.pallas import tpu as pltpu
from jax.sharding import Mesh, PartitionSpec as P

HEADS = 8
DK = 128
GROUP = 64
HALF = HEADS // 2
WIDTH = HALF * DK
QUART = WIDTH // 2
TOK = 128
PAIR = 2 * TOK
BLOCKS = PAIR // GROUP
MODEL = 2048
RANK = 16
ZS = 8
PS = 16
ROWS = HALF * DK // PS
F32 = jnp.float32
BF16 = jnp.bfloat16
XY = ("x", "y")
SWAP = ((0, 1), (1, 0))
MB = 1 << 20


def shape(dims, dtype=F32):
    return jax.ShapeDtypeStruct(dims, dtype)


BIG = 56
KEYS = 16


VM = pl.BlockSpec(memory_space=pltpu.VMEM)
ANY = pl.BlockSpec(memory_space=pl.ANY)


def kernel(body, outs, name, limit, scratch=(), specs=None, out_specs=None, alias=None):
    extra = {} if specs is None else {"in_specs": specs, "out_specs": out_specs}
    if alias:
        extra["input_output_aliases"] = alias
    return pl.pallas_call(
        body,
        out_shape=outs,
        name=name,
        scratch_shapes=scratch,
        compiler_params=pltpu.CompilerParams(vmem_limit_bytes=limit * MB),
        **extra,
    )


def split(a):
    hi = a.astype(BF16)
    return hi, (a - hi.astype(F32)).astype(BF16)


def dot(a, b, dims=((1,), (0,))):
    return lax.dot_general(a, b, (dims, ((), ())), preferred_element_type=F32)


NT = ((1,), (1,))
TN = ((0,), (0,))


def dot_hl(a, b, dims=((1,), (0,))):
    hi, lo = split(b)
    return dot(a, hi, dims) + dot(a, lo, dims)


def dot_ff(a, b, dims=((1,), (0,))):
    ah, al = split(a)
    bh, bl = split(b)
    return dot(ah, bh, dims) + dot(ah, bl, dims) + dot(al, bh, dims)


def dot_mask(mask, b):
    hi, lo = split(b)
    rest = (b - hi.astype(F32) - lo.astype(F32)).astype(BF16)
    return dot(mask, hi) + dot(mask, lo) + dot(mask, rest)


def is_first():
    return lax.axis_index("c") == 0


def pick(first, a, b):
    return jnp.where(first, a, b)


def low_mask():
    rows = lax.broadcasted_iota(jnp.int32, (GROUP, GROUP), 0)
    cols = lax.broadcasted_iota(jnp.int32, (GROUP, GROUP), 1)
    return rows >= cols, rows <= cols


def tok_of(n):
    return slice(n * GROUP, (n + 1) * GROUP)


def col_of(h):
    return slice(h * DK, (h + 1) * DK)


def span_of(beta, n):
    return beta[(n + 1) * GROUP - 1 : (n + 1) * GROUP]


def gates_body(own, peer, down, up, bias, q, g, v, q_p, g_p, v_p,
               tok, lat, logit, beta, q_o, g_o, v_o, adds, start):
    first = is_first()
    tok[:TOK] = pick(first, own[...], peer[...])
    tok[TOK:] = pick(first, peer[...], own[...])
    for ref, other, out in ((q, q_p, q_o), (g, g_p, g_o), (v, v_p, v_o)):
        mine = pick(first, ref[:, :WIDTH], ref[:, WIDTH:])
        theirs = pick(first, other[:, :WIDTH], other[:, WIDTH:])
        out[:TOK] = pick(first, mine, theirs)
        out[TOK:] = pick(first, theirs, mine)
    latent = dot(tok[...], down[...], NT).astype(BF16)
    lat[...] = latent
    up_half = pick(first, up[:, :WIDTH], up[:, WIDTH:])
    bias_half = pick(first, bias[:, :WIDTH], bias[:, WIDTH:])
    x = dot(latent, up_half) + bias_half
    logit[...] = x
    gamma = (jnp.minimum(x, 0.0) - jnp.log1p(jnp.exp(-jnp.abs(x)))) * (1.0 / 16.0)
    lower = low_mask()[0].astype(BF16)
    run = [jnp.zeros((DK, DK), F32)] * HALF
    total = jnp.zeros((1, WIDTH), F32)
    for n in reversed(range(BLOCKS)):
        b = dot_mask(lower, gamma[tok_of(n)])
        beta[tok_of(n)] = b
        last = b[GROUP - 1 : GROUP]
        total = total + last
        decay = jnp.exp(last)
        scaled = q_o[tok_of(n)].astype(F32) * jnp.exp(b)
        grad = g_o[tok_of(n)]
        for h in range(HALF):
            part = dot_hl(grad[:, col_of(h)], scaled[:, col_of(h)], TN)
            adds[n, col_of(h)] = part
            run[h] = decay[:, col_of(h)] * run[h] + part
    decay = jnp.exp(total)
    for p in range(PS):
        h, at = p // PER, (p % PER) * ROWS
        start[p, :ROWS] = run[h][at : at + ROWS]
        start[p, ROWS:] = jnp.broadcast_to(decay[:, col_of(h)], (8, DK))


def unpack_w(recv, w):
    for p in range(PS):
        for z in range(ZS):
            w[z * 256 + p * 16 : z * 256 + p * 16 + 16] = recv[p, z * 16 : z * 16 + 16]


def added_states(key, v, beta, n):
    b = beta[tok_of(n)]
    last = b[GROUP - 1 : GROUP]
    tail = key[tok_of(n)].astype(F32) * jnp.exp(last - b)
    vals = v[tok_of(n)]
    return [dot_hl(vals[:, col_of(h)], tail[:, col_of(h)], TN) for h in range(HALF)], jnp.exp(last)


def keys_body(recv, tok, beta, v, start, key_o, send, w):
    unpack_w(recv, w)
    key_o[...] = dot(tok[...], w[...]).astype(BF16)
    run = [jnp.zeros((DK, DK), F32)] * HALF
    for n in range(BLOCKS):
        parts, decay = added_states(key_o, v, beta, n)
        run = [decay[:, col_of(h)] * run[h] + parts[h] for h in range(HALF)]
    for p in range(PS):
        h, at = p // PER, (p % PER) * ROWS
        send[p, : ROWS + 8] = start[p]
        send[p, ROWS + 8 :] = run[h][at : at + ROWS]


def scan_body(recv, send):
    run = jnp.zeros((ROWS, DK), F32)
    for p in reversed(range(PS)):
        send[p, :ROWS] = run
        run = recv[p, ROWS : ROWS + 1] * run + recv[p, :ROWS]
    run = jnp.zeros((ROWS, DK), F32)
    for p in range(PS):
        send[p, ROWS:] = run
        run = recv[p, ROWS : ROWS + 1] * run + recv[p, ROWS + 8 :]


def inner_body(q_r, g_r, v_r, key_r, beta, kd_o, local):
    low, high = low_mask()
    for n in range(BLOCKS):
        b = beta[tok_of(n)]
        grow, shrink = jnp.exp(b), jnp.exp(-b)
        q = q_r[tok_of(n)].astype(F32)
        k = key_r[tok_of(n)].astype(F32)
        q_s, k_s = q * grow, k * shrink
        for h in range(HALF):
            c = col_of(h)
            g, v = g_r[tok_of(n), c], v_r[tok_of(n), c]
            pairs = jnp.where(low, dot(g, v, NT), 0.0)
            pairs_t = jnp.where(high, dot(v, g, NT), 0.0)
            kd = shrink[:, c] * dot_ff(pairs_t, q_s[:, c])
            qd = grow[:, c] * dot_ff(pairs, k_s[:, c])
            kd_o[tok_of(n), c] = kd
            local[tok_of(n), c] = q[:, c] * qd - k[:, c] * kd


def gate_body(recv, adds, key_r, v_r, beta, q_r, g_r, kd_in, local, logit, lat, up,
              kd_o, kd_keep, kd_give, gate_o, gate_keep, gate_give, up_part, lat_part, delta):
    first = is_first()
    high = low_mask()[1].astype(BF16)
    back = [jnp.concatenate([recv[h * PER + i, :ROWS] for i in range(PER)], axis=0)
            for h in range(HALF)]
    run = [jnp.concatenate([recv[h * PER + i, ROWS:] for i in range(PER)], axis=0)
           for h in range(HALF)]
    grads = list(back)
    for n in reversed(range(BLOCKS)):
        b = beta[tok_of(n)]
        last = b[GROUP - 1 : GROUP]
        decay = jnp.exp(last)
        kd = jnp.concatenate(
            [dot_hl(v_r[tok_of(n), col_of(h)], grads[h]) for h in range(HALF)], axis=1
        ) * jnp.exp(last - b)
        kd_o[tok_of(n)] = (kd + kd_in[tok_of(n)]).astype(BF16)
        delta[tok_of(n)] = local[tok_of(n)] - key_r[tok_of(n)].astype(F32) * kd
        grads = [decay[:, col_of(h)] * grads[h] + adds[n, col_of(h)] for h in range(HALF)]
    for n in range(BLOCKS):
        parts, decay = added_states(key_r, v_r, beta, n)
        qd = jnp.concatenate(
            [dot_hl(g_r[tok_of(n), col_of(h)], run[h]) for h in range(HALF)], axis=1
        ) * jnp.exp(beta[tok_of(n)])
        delta[tok_of(n)] += q_r[tok_of(n)].astype(F32) * qd
        run = [decay[:, col_of(h)] * run[h] + parts[h] for h in range(HALF)]
    odd = lax.rem(lax.axis_index("z"), 2) == 1
    kd_lo, kd_hi = kd_o[:, :QUART], kd_o[:, QUART:]
    kd_keep[...] = pick(odd, kd_hi, kd_lo)
    kd_give[...] = pick(odd, kd_lo, kd_hi)
    beyond = jnp.concatenate(
        [jnp.sum(run[h] * back[h], axis=0, keepdims=True) for h in range(HALF)], axis=1
    )
    for n in reversed(range(BLOCKS)):
        suffix = dot_mask(high, delta[tok_of(n)]) + beyond
        beyond = suffix[:1]
        x = logit[tok_of(n)]
        gate_o[tok_of(n)] = (suffix * (1.0 / (1.0 + jnp.exp(x))) * (1.0 / 16.0)).astype(BF16)
    gate = gate_o[...]
    gate_keep[...] = pick(first, gate[:TOK], gate[TOK:])
    gate_give[...] = pick(first, gate[TOK:], gate[:TOK])
    up_half = pick(first, up[:, :WIDTH], up[:, WIDTH:])
    up_part[...] = dot(lat[...], gate, TN)
    lat_part[...] = dot(gate, up_half, NT)


SMALL = 3 * RANK


def down_body(lat_a, lat_b, tok, up_part, lat_o, both):
    first = is_first()
    latent = (lat_a[...] + lat_b[...]).astype(BF16)
    lat_o[...] = pick(first, latent[:TOK], latent[TOK:])
    half = MODEL // 2
    down = dot(latent, pick(first, tok[:, :half], tok[:, half:]), TN)
    both[...] = jnp.concatenate(
        [up_part[...], down[:, :WIDTH], down[:, WIDTH:]], axis=0
    ).astype(BF16)


def weight_body(tok, kd_r, far, far_peer, far_kd, small, send):
    first = is_first()
    kd, kd_far = kd_r[...], far_kd[...]
    kd_a = pick(first, kd_far[:TOK], kd_far[TOK:])
    kd_b = pick(first, kd_far[TOK:], kd_far[:TOK])
    for z in range(ZS):
        cols = slice(z * 256, z * 256 + 256)
        block = dot(tok[:, cols], kd, TN)
        block = block + dot(far[:, cols], kd_a, TN) + dot(far_peer[:, cols], kd_b, TN)
        block = block.astype(BF16)
        at, lane = SMALL + (z % 4) * 16, (z // 4) * QUART
        for p in range(PS):
            send[p, at : at + 16, lane : lane + QUART] = block[p * 16 : p * 16 + 16]
    few = small[...]
    for p in range(PS):
        send[p, :SMALL] = few


def through_body(kd, recv, keep, give, w):
    first = is_first()
    unpack_w(recv, w)
    mine = pick(first, kd[:TOK], kd[TOK:])
    other = pick(first, kd[TOK:], kd[:TOK])
    give[...] = dot(other, w[...], NT)
    keep[...] = dot(mine, w[...], NT)


def input_body(keep, got, lat, down, out):
    out[...] = (keep[...] + got[...] + dot(lat[...], down[...])).astype(BF16)


PER = DK // ROWS


def plane_body(recv, send):
    total = jnp.sum(recv[...].astype(F32), axis=0).astype(BF16)
    for z in range(ZS):
        at, lane = SMALL + (z % 4) * 16, (z // 4) * QUART
        send[z, :SMALL] = total[:SMALL]
        send[z, SMALL:, :QUART] = total[at : at + 16, lane : lane + QUART]
        send[z, SMALL:, QUART:] = jnp.zeros((16, QUART), BF16)


def total_body(recv, keep, give):
    first = is_first()
    small = jnp.sum(recv[:, :SMALL].astype(F32), axis=0)
    parts = [recv[z, SMALL:, :QUART].astype(F32) for z in range(ZS)]
    rows = jnp.concatenate([sum(parts[0::2]), sum(parts[1::2])], axis=1)
    keep[...] = jnp.concatenate([small, pick(first, rows[:8], rows[8:])], axis=0)
    give[...] = jnp.concatenate([small, pick(first, rows[8:], rows[:8])], axis=0)


def out_body(mine, theirs, down_o, up_o, w_o):
    first = is_first()
    halves = (pick(first, mine[...], theirs[...]), pick(first, theirs[...], mine[...]))
    for i, a in enumerate(halves):
        up_o[:, i * WIDTH : (i + 1) * WIDTH] = a[:RANK]
        down_o[:, 2 * i * WIDTH : (2 * i + 1) * WIDTH] = a[RANK : 2 * RANK]
        down_o[:, (2 * i + 1) * WIDTH : (2 * i + 2) * WIDTH] = a[2 * RANK : 3 * RANK]
        w_o[:, i * WIDTH : (i + 1) * WIDTH] = a[3 * RANK :]


def swap(a):
    return lax.ppermute(a, "c", SWAP)


def across(a):
    return lax.ppermute(a, "z", [(i, i ^ 1) for i in range(ZS)])


def a2a(a, axis):
    return lax.all_to_all(a, axis, 0, 0)


def local(inputs, queries, values, out_grad, key_weight, gate_down, gate_up, gate_bias):
    first = is_first()
    own = inputs[0]
    q, g, v = queries[0], out_grad[0], values[0]
    half_bf = shape((PAIR, WIDTH), BF16)
    half_f = shape((PAIR, WIDTH))
    packed = shape((PS, ROWS + 8, DK))

    lo, hi = key_weight[:, :WIDTH], key_weight[:, WIDTH:]
    w_m, w_p = jnp.where(first, lo, hi), swap(jnp.where(first, hi, lo))
    w_chip = jnp.concatenate([jnp.where(first, w_m, w_p), jnp.where(first, w_p, w_m)], axis=0)
    w_z = a2a(jnp.broadcast_to(w_chip[None], (ZS, 16, WIDTH)), "z").reshape(ZS * 16, WIDTH)
    w_all = a2a(jnp.broadcast_to(w_z[None], (PS, ZS * 16, WIDTH)), XY)

    tok, lat, logit, beta, q, g, v, add_g, start = kernel(
        gates_body,
        (shape((PAIR, MODEL), BF16), shape((PAIR, RANK), BF16), half_f, half_f,
         half_bf, half_bf, half_bf, shape((BLOCKS, WIDTH, DK)), packed),
        "gates", BIG,
    )(own, swap(own), gate_down, gate_up, gate_bias[None], q, g, v, swap(q), swap(g), swap(v))
    far = across(own)
    far_peer = swap(far)
    keys, send = kernel(
        keys_body, (half_bf, shape((PS, 2 * ROWS + 8, DK))), "keys", KEYS,
        scratch=[pltpu.VMEM((MODEL, WIDTH), BF16)],
    )(w_all, tok, beta, v, start)
    recv = a2a(send, XY)
    kd_local, local_part = kernel(inner_body, (half_f, half_f), "inner", BIG)(q, g, v, keys, beta)
    recv = a2a(kernel(scan_body, shape((PS, 2 * ROWS, DK)), "scan", 8)(recv), XY)
    quarter = shape((PAIR, QUART), BF16)
    kd, kd_keep, kd_give, gate, gate_m, gate_x, up_part, lat_part = kernel(
        gate_body,
        (half_bf, quarter, quarter, half_bf, shape((TOK, WIDTH), BF16),
         shape((TOK, WIDTH), BF16), shape((RANK, WIDTH)), shape((PAIR, RANK))),
        "gate", BIG, scratch=[pltpu.VMEM((PAIR, WIDTH), F32)],
    )(recv, add_g, keys, v, beta, q, g, kd_local, local_part, logit, lat, gate_up)
    far_kd = across(kd_give)
    lat_own, small = kernel(
        down_body, (shape((TOK, RANK), BF16), shape((SMALL, WIDTH), BF16)), "down", 8
    )(lat_part, swap(lat_part), tok, up_part)
    send = kernel(
        weight_body, shape((PS, SMALL + ZS * 8, WIDTH), BF16), "weights", BIG
    )(tok, kd_keep, far, far_peer, far_kd, small)
    send = kernel(plane_body, shape((ZS, SMALL + 16, WIDTH), BF16), "plane", 8)(a2a(send, XY))
    end = shape((SMALL + 8, WIDTH))
    keep, give = kernel(total_body, (end, end), "total", 8)(a2a(send, "z"))
    down_grad, up_grad, key_weight_grad = kernel(
        out_body,
        (shape((RANK, MODEL)), shape((RANK, 2 * WIDTH)), shape((8, 2 * WIDTH))), "grads", 8,
    )(keep, swap(give))

    gate_p = swap(gate_x)
    gate_grad = jnp.concatenate(
        [jnp.where(first, gate_m, gate_p), jnp.where(first, gate_p, gate_m)], axis=1
    )
    mine, other = kernel(
        through_body, (shape((TOK, MODEL)), shape((TOK, MODEL))), "through", BIG,
        scratch=[pltpu.VMEM((MODEL, WIDTH), BF16)],
    )(kd, w_all)
    input_grad = kernel(input_body, shape((TOK, MODEL), BF16), "input", 16)(
        mine, swap(other), lat_own, gate_down
    )
    return (input_grad[None], gate_grad[None], key_weight_grad, down_grad, up_grad)


def solution(mesh):
    grid = Mesh(mesh.devices.reshape(8, 4, 4, 2), ("z", "x", "y", "c"))
    seq = ("x", "y", "c")
    tok = P("z", seq, None)
    row = P(("z",) + seq, None)
    return jax.shard_map(
        local,
        mesh=grid,
        in_specs=(tok, tok, tok, tok, row, P(), P(), P()),
        out_specs=(tok, tok, row, P(), P()),
        check_vma=False,
    )
```

```python
import jax
import jax.numpy as jnp
from jax import lax
from jax.experimental import pallas as pl
from jax.experimental.pallas import tpu as pltpu
from jax.sharding import Mesh, PartitionSpec as P

HEADS = 8
DK = 128
GROUP = 64
HALF = HEADS // 2
WIDTH = HALF * DK
QUART = WIDTH // 2
TOK = 128
PAIR = 2 * TOK
BLOCKS = PAIR // GROUP
MODEL = 2048
RANK = 16
ZS = 8
PS = 16
ROWS = HALF * DK // PS
F32 = jnp.float32
BF16 = jnp.bfloat16
XY = ("x", "y")
SWAP = ((0, 1), (1, 0))
MB = 1 << 20


def shape(dims, dtype=F32):
    return jax.ShapeDtypeStruct(dims, dtype)


BIG = 56
KEYS = 16


VM = pl.BlockSpec(memory_space=pltpu.VMEM)
HBM = pl.BlockSpec(memory_space=pltpu.HBM)


def kernel(body, outs, name, limit, scratch=(), specs=None, out_specs=None, alias=None):
    extra = {} if specs is None else {"in_specs": specs, "out_specs": out_specs}
    if alias:
        extra["input_output_aliases"] = alias
    return pl.pallas_call(
        body,
        out_shape=outs,
        name=name,
        scratch_shapes=scratch,
        compiler_params=pltpu.CompilerParams(vmem_limit_bytes=limit * MB),
        **extra,
    )


def split(a):
    hi = a.astype(BF16)
    return hi, (a - hi.astype(F32)).astype(BF16)


def dot(a, b, dims=((1,), (0,))):
    return lax.dot_general(a, b, (dims, ((), ())), preferred_element_type=F32)


NT = ((1,), (1,))
TN = ((0,), (0,))


def dot_hl(a, b, dims=((1,), (0,))):
    hi, lo = split(b)
    return dot(a, hi, dims) + dot(a, lo, dims)


def dot_ff(a, b, dims=((1,), (0,))):
    ah, al = split(a)
    bh, bl = split(b)
    return dot(ah, bh, dims) + dot(ah, bl, dims) + dot(al, bh, dims)


def dot_mask(mask, b):
    hi, lo = split(b)
    rest = (b - hi.astype(F32) - lo.astype(F32)).astype(BF16)
    return dot(mask, hi) + dot(mask, lo) + dot(mask, rest)


def is_first():
    return lax.axis_index("c") == 0


def pick(first, a, b):
    return jnp.where(first, a, b)


def low_mask():
    rows = lax.broadcasted_iota(jnp.int32, (GROUP, GROUP), 0)
    cols = lax.broadcasted_iota(jnp.int32, (GROUP, GROUP), 1)
    return rows >= cols, rows <= cols


def tok_of(n):
    return slice(n * GROUP, (n + 1) * GROUP)


def col_of(h):
    return slice(h * DK, (h + 1) * DK)


def span_of(beta, n):
    return beta[(n + 1) * GROUP - 1 : (n + 1) * GROUP]


def gates_body(own, peer, down, up, bias, q, g, v, q_p, g_p, v_p,
               tok, lat, logit, beta, q_o, g_o, v_o, adds, start):
    first = is_first()
    tok[:TOK] = pick(first, own[...], peer[...])
    tok[TOK:] = pick(first, peer[...], own[...])
    for ref, other, out in ((q, q_p, q_o), (g, g_p, g_o), (v, v_p, v_o)):
        mine = pick(first, ref[:, :WIDTH], ref[:, WIDTH:])
        theirs = pick(first, other[:, :WIDTH], other[:, WIDTH:])
        out[:TOK] = pick(first, mine, theirs)
        out[TOK:] = pick(first, theirs, mine)
    latent = dot(tok[...], down[...], NT).astype(BF16)
    lat[...] = latent
    up_half = pick(first, up[:, :WIDTH], up[:, WIDTH:])
    bias_half = pick(first, bias[:, :WIDTH], bias[:, WIDTH:])
    x = dot(latent, up_half) + bias_half
    logit[...] = x
    gamma = (jnp.minimum(x, 0.0) - jnp.log1p(jnp.exp(-jnp.abs(x)))) * (1.0 / 16.0)
    lower = low_mask()[0].astype(BF16)
    run = [jnp.zeros((DK, DK), F32)] * HALF
    total = jnp.zeros((1, WIDTH), F32)
    for n in reversed(range(BLOCKS)):
        b = dot_mask(lower, gamma[tok_of(n)])
        beta[tok_of(n)] = b
        last = b[GROUP - 1 : GROUP]
        total = total + last
        decay = jnp.exp(last)
        scaled = q_o[tok_of(n)].astype(F32) * jnp.exp(b)
        grad = g_o[tok_of(n)]
        for h in range(HALF):
            part = dot_hl(grad[:, col_of(h)], scaled[:, col_of(h)], TN)
            adds[n, col_of(h)] = part
            run[h] = decay[:, col_of(h)] * run[h] + part
    decay = jnp.exp(total)
    for p in range(PS):
        h, at = p // PER, (p % PER) * ROWS
        start[p, :ROWS] = run[h][at : at + ROWS].astype(BF16)
        row = decay[:, col_of(h)]
        top = row.astype(BF16).astype(F32)
        start[p, ROWS:] = jnp.concatenate(
            [jnp.broadcast_to(top, (8, DK)), jnp.broadcast_to(row - top, (8, DK))], axis=0
        ).astype(BF16)


def added_states(key, v, beta, n):
    b = beta[tok_of(n)]
    last = b[GROUP - 1 : GROUP]
    tail = key[tok_of(n)].astype(F32) * jnp.exp(last - b)
    vals = v[tok_of(n)]
    return [dot_hl(vals[:, col_of(h)], tail[:, col_of(h)], TN) for h in range(HALF)], jnp.exp(last)


def load(pairs, sems):
    copies = [pltpu.make_async_copy(a, b, sems.at[i]) for i, (a, b) in enumerate(pairs)]
    for copy in copies:
        copy.start()
    return copies


def far_keys_body(recv, far, far_peer, _, key_o, w, a, b, sems):
    copies = load(((far, a), (far_peer, b)), sems)
    for p in range(PS):
        for z in range(ZS):
            w[z * 256 + p * 16 : z * 256 + p * 16 + 16] = recv[p, z * 16 : z * 16 + 16]
    for copy in copies:
        copy.wait()
    first = is_first()
    key_a, key_b = dot(a[...], w[...]), dot(b[...], w[...])
    key_o[:TOK] = pick(first, key_a, key_b).astype(BF16)
    key_o[TOK:] = pick(first, key_b, key_a).astype(BF16)


def near_keys_body(tok, w, key_o):
    key_o[...] = dot(tok[...], w[...]).astype(BF16)


def odd_z():
    return lax.rem(lax.axis_index("z"), 2) == 1


def keys_body(mine, theirs, beta_h, v_h, start, _, key_o, send, w_o, beta, v, sems):
    copies = load(((beta_h, beta), (v_h, v)), sems)
    odd = odd_z()
    key_o[:, :QUART] = pick(odd, theirs[...], mine[...])
    key_o[:, QUART:] = pick(odd, mine[...], theirs[...])
    for copy in copies:
        copy.wait()
    run = [jnp.zeros((DK, DK), F32)] * HALF
    for n in range(BLOCKS):
        parts, decay = added_states(key_o, v, beta, n)
        run = [decay[:, col_of(h)] * run[h] + parts[h] for h in range(HALF)]
    for p in range(PS):
        h, at = p // PER, (p % PER) * ROWS
        send[p, : ROWS + 16] = start[p]
        send[p, ROWS + 16 :] = run[h][at : at + ROWS].astype(BF16)


def scan_body(recv, send):
    def decay(p):
        rows = recv[p, ROWS : ROWS + 16].astype(F32)
        return rows[:1] + rows[8:9]

    run = jnp.zeros((ROWS, DK), F32)
    for p in reversed(range(PS)):
        send[p, :ROWS] = run.astype(BF16)
        run = decay(p) * run + recv[p, :ROWS].astype(F32)
    run = jnp.zeros((ROWS, DK), F32)
    for p in range(PS):
        send[p, ROWS:] = run.astype(BF16)
        run = decay(p) * run + recv[p, ROWS + 16 :].astype(F32)


def inner_body(q_r, g_r, v_r, key_r, beta, kd_o, local):
    low, high = low_mask()
    for n in range(BLOCKS):
        b = beta[tok_of(n)]
        grow, shrink = jnp.exp(b), jnp.exp(-b)
        q = q_r[tok_of(n)].astype(F32)
        k = key_r[tok_of(n)].astype(F32)
        q_s, k_s = q * grow, k * shrink
        for h in range(HALF):
            c = col_of(h)
            g, v = g_r[tok_of(n), c], v_r[tok_of(n), c]
            pairs = jnp.where(low, dot(g, v, NT), 0.0)
            pairs_t = jnp.where(high, dot(v, g, NT), 0.0)
            kd = shrink[:, c] * dot_ff(pairs_t, q_s[:, c])
            qd = grow[:, c] * dot_ff(pairs, k_s[:, c])
            kd_o[tok_of(n), c] = kd
            local[tok_of(n), c] = q[:, c] * qd - k[:, c] * kd


def gate_body(recv, adds, key_r, v_r, beta, q_r, g_r, kd_in, local, logit, lat, up, _,
              kd_o, kd_keep, kd_give, gate_o, gate_keep, gate_give, up_part, lat_part, delta):
    first = is_first()
    high = low_mask()[1].astype(BF16)
    back = [jnp.concatenate([recv[h * PER + i, :ROWS] for i in range(PER)], axis=0).astype(F32)
            for h in range(HALF)]
    run = [jnp.concatenate([recv[h * PER + i, ROWS:] for i in range(PER)], axis=0).astype(F32)
           for h in range(HALF)]
    grads = list(back)
    for n in reversed(range(BLOCKS)):
        b = beta[tok_of(n)]
        last = b[GROUP - 1 : GROUP]
        decay = jnp.exp(last)
        kd = jnp.concatenate(
            [dot_hl(v_r[tok_of(n), col_of(h)], grads[h]) for h in range(HALF)], axis=1
        ) * jnp.exp(last - b)
        kd_o[tok_of(n)] = (kd + kd_in[tok_of(n)]).astype(BF16)
        delta[tok_of(n)] = local[tok_of(n)] - key_r[tok_of(n)].astype(F32) * kd
        grads = [decay[:, col_of(h)] * grads[h] + adds[n, col_of(h)] for h in range(HALF)]
    for n in range(BLOCKS):
        parts, decay = added_states(key_r, v_r, beta, n)
        qd = jnp.concatenate(
            [dot_hl(g_r[tok_of(n), col_of(h)], run[h]) for h in range(HALF)], axis=1
        ) * jnp.exp(beta[tok_of(n)])
        delta[tok_of(n)] += q_r[tok_of(n)].astype(F32) * qd
        run = [decay[:, col_of(h)] * run[h] + parts[h] for h in range(HALF)]
    odd = odd_z()
    kd_lo, kd_hi = kd_o[:, :QUART], kd_o[:, QUART:]
    kd_keep[...] = pick(odd, kd_hi, kd_lo)
    kd_give[...] = pick(odd, kd_lo, kd_hi)
    beyond = jnp.concatenate(
        [jnp.sum(run[h] * back[h], axis=0, keepdims=True) for h in range(HALF)], axis=1
    )
    for n in reversed(range(BLOCKS)):
        suffix = dot_mask(high, delta[tok_of(n)]) + beyond
        beyond = suffix[:1]
        x = logit[tok_of(n)]
        gate_o[tok_of(n)] = (suffix * (1.0 / (1.0 + jnp.exp(x))) * (1.0 / 16.0)).astype(BF16)
    gate = gate_o[...]
    gate_keep[...] = pick(first, gate[:TOK], gate[TOK:])
    gate_give[...] = pick(first, gate[TOK:], gate[:TOK])
    up_half = pick(first, up[:, :WIDTH], up[:, WIDTH:])
    up_part[...] = dot(lat[...], gate, TN)
    lat_part[...] = dot(gate, up_half, NT)


SMALL = 3 * RANK


def down_body(lat_a, lat_b, tok, up_part, lat_o, both):
    first = is_first()
    latent = (lat_a[...] + lat_b[...]).astype(BF16)
    lat_o[...] = pick(first, latent[:TOK], latent[TOK:])
    half = MODEL // 2
    down = dot(latent, pick(first, tok[:, :half], tok[:, half:]), TN)
    both[...] = jnp.concatenate(
        [up_part[...], down[:, :WIDTH], down[:, WIDTH:]], axis=0
    ).astype(BF16)


def weight_body(tok, kd_r, far, far_peer, far_kd, small, send):
    first = is_first()
    kd, kd_far = kd_r[...], far_kd[...]
    kd_a = pick(first, kd_far[:TOK], kd_far[TOK:])
    kd_b = pick(first, kd_far[TOK:], kd_far[:TOK])
    for z in range(ZS):
        cols = slice(z * 256, z * 256 + 256)
        block = dot(tok[:, cols], kd, TN)
        block = block + dot(far[:, cols], kd_a, TN) + dot(far_peer[:, cols], kd_b, TN)
        block = block.astype(BF16)
        at, lane = SMALL + (z % 4) * 16, (z // 4) * QUART
        for p in range(PS):
            send[p, at : at + 16, lane : lane + QUART] = block[p * 16 : p * 16 + 16]
    few = small[...]
    for p in range(PS):
        send[p, :SMALL] = few


def through_body(kd, kd_far, w, w_far, keep, give):
    first = is_first()
    total = dot(kd[...], w[...], NT) + dot(kd_far[...], w_far[...], NT)
    give[...] = pick(first, total[TOK:], total[:TOK])
    keep[...] = pick(first, total[:TOK], total[TOK:])


def input_body(keep, got, lat, down, out):
    out[...] = (keep[...] + got[...] + dot(lat[...], down[...])).astype(BF16)


PER = DK // ROWS


def plane_body(recv, send):
    total = jnp.sum(recv[...].astype(F32), axis=0).astype(BF16)
    for z in range(ZS):
        at, lane = SMALL + (z % 4) * 16, (z // 4) * QUART
        send[z, :SMALL] = total[:SMALL]
        send[z, SMALL:, :QUART] = total[at : at + 16, lane : lane + QUART]
        send[z, SMALL:, QUART:] = jnp.zeros((16, QUART), BF16)


def total_body(recv, a, b, keep, give):
    first = is_first()
    small = jnp.sum(recv[:, :SMALL].astype(F32), axis=0)
    parts = [recv[z, SMALL:, :QUART].astype(F32) for z in range(ZS)]
    rows = jnp.concatenate([sum(parts[0::2]), sum(parts[1::2])], axis=1)
    keep[...] = jnp.concatenate([small, pick(first, rows[:8], rows[8:])], axis=0)
    give[...] = jnp.concatenate([small, pick(first, rows[8:], rows[:8])], axis=0)


def out_body(mine, theirs, down_o, up_o, w_o):
    first = is_first()
    halves = (pick(first, mine[...], theirs[...]), pick(first, theirs[...], mine[...]))
    for i, a in enumerate(halves):
        up_o[:, i * WIDTH : (i + 1) * WIDTH] = a[:RANK]
        down_o[:, 2 * i * WIDTH : (2 * i + 1) * WIDTH] = a[RANK : 2 * RANK]
        down_o[:, (2 * i + 1) * WIDTH : (2 * i + 2) * WIDTH] = a[2 * RANK : 3 * RANK]
        w_o[:, i * WIDTH : (i + 1) * WIDTH] = a[3 * RANK :]


def swap(a):
    return lax.ppermute(a, "c", SWAP)


def across(a):
    return lax.ppermute(a, "z", [(i, i ^ 1) for i in range(ZS)])


def a2a(a, axis):
    return lax.all_to_all(a, axis, 0, 0)


def local(inputs, queries, values, out_grad, key_weight, gate_down, gate_up, gate_bias):
    first = is_first()
    own = inputs[0]
    q, g, v = queries[0], out_grad[0], values[0]
    half_bf = shape((PAIR, WIDTH), BF16)
    half_f = shape((PAIR, WIDTH))
    packed = shape((PS, ROWS + 16, DK), BF16)
    quarter = shape((PAIR, QUART), BF16)

    lo, hi = key_weight[:, :WIDTH], key_weight[:, WIDTH:]
    w_m, w_p = jnp.where(first, lo, hi), swap(jnp.where(first, hi, lo))
    w_chip = jnp.concatenate([jnp.where(first, w_m, w_p), jnp.where(first, w_p, w_m)], axis=0)
    w_two = jnp.stack([w_chip[:, :QUART], w_chip[:, QUART:]])
    w_z = jnp.broadcast_to(w_two[None], (ZS // 2, 2, 16, QUART)).reshape(ZS, 16, QUART)
    w_z = a2a(w_z, "z").reshape(ZS * 16, QUART)
    w_all = a2a(jnp.broadcast_to(w_z[None], (PS, ZS * 16, QUART)), XY)

    tok, lat, logit, beta, q, g, v, add_g, start = kernel(
        gates_body,
        (shape((PAIR, MODEL), BF16), shape((PAIR, RANK), BF16), half_f, half_f,
         half_bf, half_bf, half_bf, shape((BLOCKS, WIDTH, DK)), packed),
        "gates", BIG,
    )(own, swap(own), gate_down, gate_up, gate_bias[None], q, g, v, swap(q), swap(g), swap(v))
    far = across(own)
    far_peer = swap(far)
    tok_sems = pltpu.SemaphoreType.DMA((2,))
    keys_far, w = kernel(
        far_keys_body, (quarter, shape((MODEL, QUART), BF16)), "far_keys", 16,
        specs=[VM, HBM, HBM, HBM], out_specs=(VM, VM),
        scratch=[pltpu.VMEM((TOK, MODEL), BF16)] * 2 + [tok_sems],
    )(w_all, far, far_peer, beta)
    keys_mine = kernel(near_keys_body, quarter, "near_keys", 16)(tok, w)
    keys, send, w = kernel(
        keys_body,
        (half_bf, shape((PS, 2 * ROWS + 16, DK), BF16), shape((MODEL, QUART), BF16)),
        "keys", 16, specs=[VM, VM, HBM, HBM, VM, HBM], out_specs=(VM, VM, HBM), alias={5: 2},
        scratch=[pltpu.VMEM((PAIR, WIDTH), F32), pltpu.VMEM((PAIR, WIDTH), BF16), tok_sems],
    )(keys_mine, across(keys_far), beta, v, start, w)
    w_far = across(w)
    recv = a2a(send, XY)
    kd_local, local_part = kernel(inner_body, (half_f, half_f), "inner", BIG)(q, g, v, keys, beta)
    recv = a2a(kernel(scan_body, shape((PS, 2 * ROWS, DK), BF16), "scan", 8)(recv), XY)
    kd, kd_keep, kd_give, gate, gate_m, gate_x, up_part, lat_part = kernel(
        gate_body,
        (half_bf, quarter, quarter, half_bf, shape((TOK, WIDTH), BF16),
         shape((TOK, WIDTH), BF16), shape((RANK, WIDTH)), shape((PAIR, RANK))),
        "gate", BIG, scratch=[pltpu.VMEM((PAIR, WIDTH), F32)],
        specs=[VM] * 12 + [HBM], out_specs=(VM,) * 8,
    )(recv, add_g, keys, v, beta, q, g, kd_local, local_part, logit, lat, gate_up, w_far)
    far_kd = across(kd_give)
    lat_own, small = kernel(
        down_body, (shape((TOK, RANK), BF16), shape((SMALL, WIDTH), BF16)), "down", 8
    )(lat_part, swap(lat_part), tok, up_part)
    send = kernel(
        weight_body, shape((PS, SMALL + ZS * 8, WIDTH), BF16), "weights", BIG
    )(tok, kd_keep, far, far_peer, far_kd, small)
    send = kernel(plane_body, shape((ZS, SMALL + 16, WIDTH), BF16), "plane", 8)(a2a(send, XY))
    gate_p = swap(gate_x)
    gate_grad = jnp.concatenate(
        [jnp.where(first, gate_m, gate_p), jnp.where(first, gate_p, gate_m)], axis=1
    )
    mine, other = kernel(
        through_body, (shape((TOK, MODEL)), shape((TOK, MODEL))), "through", BIG
    )(kd_keep, kd_give, w, w_far)
    input_grad = kernel(input_body, shape((TOK, MODEL), BF16), "input", BIG)(
        mine, swap(other), lat_own, gate_down
    )
    end = shape((SMALL + 8, WIDTH))
    keep, give = kernel(
        total_body, (end, end), "total", 8, specs=[VM, HBM, HBM], out_specs=(VM, VM)
    )(a2a(send, "z"), input_grad, gate_grad)
    down_grad, up_grad, key_weight_grad = kernel(
        out_body,
        (shape((RANK, MODEL)), shape((RANK, 2 * WIDTH)), shape((8, 2 * WIDTH))), "grads", 8,
    )(keep, swap(give))

    return (input_grad[None], gate_grad[None], key_weight_grad, down_grad, up_grad)


def solution(mesh):
    grid = Mesh(mesh.devices.reshape(8, 4, 4, 2), ("z", "x", "y", "c"))
    seq = ("x", "y", "c")
    tok = P("z", seq, None)
    row = P(("z",) + seq, None)
    return jax.shard_map(
        local,
        mesh=grid,
        in_specs=(tok, tok, tok, tok, row, P(), P(), P()),
        out_specs=(tok, tok, row, P(), P()),
        check_vma=False,
    )
```

```python
import jax
import jax.numpy as jnp
from jax import lax
from jax.experimental import pallas as pl
from jax.experimental.pallas import tpu as pltpu
from jax.sharding import Mesh, PartitionSpec as P

HEADS = 8
DK = 128
GROUP = 64
HALF = HEADS // 2
WIDTH = HALF * DK
QUART = WIDTH // 2
TOK = 128
PAIR = 2 * TOK
BLOCKS = PAIR // GROUP
MODEL = 2048
RANK = 16
ZS = 8
PS = 16
ROWS = HALF * DK // PS
F32 = jnp.float32
BF16 = jnp.bfloat16
XY = ("x", "y")
SWAP = ((0, 1), (1, 0))
MB = 1 << 20


def shape(dims, dtype=F32):
    return jax.ShapeDtypeStruct(dims, dtype)


BIG = 56
FAR = 16


VM = pl.BlockSpec(memory_space=pltpu.VMEM)
HBM = pl.BlockSpec(memory_space=pltpu.HBM)


def kernel(body, outs, name, limit, scratch=(), specs=None, out_specs=None, alias=None):
    extra = {} if specs is None else {"in_specs": specs, "out_specs": out_specs}
    if alias:
        extra["input_output_aliases"] = alias
    return pl.pallas_call(
        body,
        out_shape=outs,
        name=name,
        scratch_shapes=scratch,
        compiler_params=pltpu.CompilerParams(vmem_limit_bytes=limit * MB),
        **extra,
    )


def split(a):
    hi = a.astype(BF16)
    return hi, (a - hi.astype(F32)).astype(BF16)


def dot(a, b, dims=((1,), (0,))):
    return lax.dot_general(a, b, (dims, ((), ())), preferred_element_type=F32)


NT = ((1,), (1,))
TN = ((0,), (0,))


def dot_hl(a, b, dims=((1,), (0,))):
    hi, lo = split(b)
    return dot(a, hi, dims) + dot(a, lo, dims)


def dot_ff(a, b, dims=((1,), (0,))):
    ah, al = split(a)
    bh, bl = split(b)
    return dot(ah, bh, dims) + dot(ah, bl, dims) + dot(al, bh, dims)


def dot_mask(mask, b):
    hi, lo = split(b)
    rest = (b - hi.astype(F32) - lo.astype(F32)).astype(BF16)
    return dot(mask, hi) + dot(mask, lo) + dot(mask, rest)


def is_first():
    return lax.axis_index("c") == 0


def pick(first, a, b):
    return jnp.where(first, a, b)


def low_mask():
    rows = lax.broadcasted_iota(jnp.int32, (GROUP, GROUP), 0)
    cols = lax.broadcasted_iota(jnp.int32, (GROUP, GROUP), 1)
    return rows >= cols, rows <= cols


def tok_of(n):
    return slice(n * GROUP, (n + 1) * GROUP)


def col_of(h):
    return slice(h * DK, (h + 1) * DK)


def span_of(beta, n):
    return beta[(n + 1) * GROUP - 1 : (n + 1) * GROUP]


def gates_body(own, peer, down, up, bias, q, g, v, q_p, g_p, v_p,
               tok, lat, logit, beta, q_o, g_o, v_o, adds, start):
    first = is_first()
    tok[:TOK] = pick(first, own[...], peer[...])
    tok[TOK:] = pick(first, peer[...], own[...])
    for ref, other, out in ((q, q_p, q_o), (g, g_p, g_o), (v, v_p, v_o)):
        mine = pick(first, ref[:, :WIDTH], ref[:, WIDTH:])
        theirs = pick(first, other[:, :WIDTH], other[:, WIDTH:])
        out[:TOK] = pick(first, mine, theirs)
        out[TOK:] = pick(first, theirs, mine)
    latent = dot(tok[...], down[...], NT).astype(BF16)
    lat[...] = latent
    up_half = pick(first, up[:, :WIDTH], up[:, WIDTH:])
    bias_half = pick(first, bias[:, :WIDTH], bias[:, WIDTH:])
    x = dot(latent, up_half) + bias_half
    logit[...] = x
    gamma = (jnp.minimum(x, 0.0) - jnp.log1p(jnp.exp(-jnp.abs(x)))) * (1.0 / 16.0)
    lower = low_mask()[0].astype(BF16)
    run = [jnp.zeros((DK, DK), F32)] * HALF
    total = jnp.zeros((1, WIDTH), F32)
    for n in reversed(range(BLOCKS)):
        b = dot_mask(lower, gamma[tok_of(n)])
        beta[tok_of(n)] = b
        last = b[GROUP - 1 : GROUP]
        total = total + last
        decay = jnp.exp(last)
        scaled = q_o[tok_of(n)].astype(F32) * jnp.exp(b)
        grad = g_o[tok_of(n)]
        for h in range(HALF):
            part = dot_hl(grad[:, col_of(h)], scaled[:, col_of(h)], TN)
            adds[n, col_of(h)] = part
            run[h] = decay[:, col_of(h)] * run[h] + part
    decay = jnp.exp(total)
    for p in range(PS):
        h, at = p // PER, (p % PER) * ROWS
        start[p, :ROWS] = run[h][at : at + ROWS].astype(BF16)
        row = decay[:, col_of(h)]
        top = row.astype(BF16).astype(F32)
        start[p, ROWS:] = jnp.concatenate(
            [jnp.broadcast_to(top, (8, DK)), jnp.broadcast_to(row - top, (8, DK))], axis=0
        ).astype(BF16)


def added_states(key, v, beta, n):
    b = beta[tok_of(n)]
    last = b[GROUP - 1 : GROUP]
    tail = key[tok_of(n)].astype(F32) * jnp.exp(last - b)
    vals = v[tok_of(n)]
    return [dot_hl(vals[:, col_of(h)], tail[:, col_of(h)], TN) for h in range(HALF)], jnp.exp(last)


def load(pairs, sems):
    copies = [pltpu.make_async_copy(a, b, sems.at[i]) for i, (a, b) in enumerate(pairs)]
    for copy in copies:
        copy.start()
    return copies


def far_keys_body(recv, far, far_peer, _, key_o, w, a, b, sems):
    copies = load(((far, a), (far_peer, b)), sems)
    for p in range(PS):
        for z in range(ZS):
            w[z * 256 + p * 16 : z * 256 + p * 16 + 16] = recv[p, z * 16 : z * 16 + 16]
    for copy in copies:
        copy.wait()
    first = is_first()
    key_a, key_b = dot(a[...], w[...]), dot(b[...], w[...])
    key_o[:TOK] = pick(first, key_a, key_b).astype(BF16)
    key_o[TOK:] = pick(first, key_b, key_a).astype(BF16)


def near_keys_body(tok, w, key_o):
    key_o[...] = dot(tok[...], w[...]).astype(BF16)


def odd_z():
    return lax.rem(lax.axis_index("z"), 2) == 1


def keys_body(mine, theirs, beta_h, v_h, start, _, key_o, send, w_o, beta, v, sems):
    copies = load(((beta_h, beta), (v_h, v)), sems)
    odd = odd_z()
    key_o[:, :QUART] = pick(odd, theirs[...], mine[...])
    key_o[:, QUART:] = pick(odd, mine[...], theirs[...])
    for copy in copies:
        copy.wait()
    run = [jnp.zeros((DK, DK), F32)] * HALF
    for n in range(BLOCKS):
        parts, decay = added_states(key_o, v, beta, n)
        run = [decay[:, col_of(h)] * run[h] + parts[h] for h in range(HALF)]
    for p in range(PS):
        h, at = p // PER, (p % PER) * ROWS
        send[p, : ROWS + 16] = start[p]
        send[p, ROWS + 16 :] = run[h][at : at + ROWS].astype(BF16)


def scan_body(recv, send):
    def decay(p):
        rows = recv[p, ROWS : ROWS + 16].astype(F32)
        return rows[:1] + rows[8:9]

    run = jnp.zeros((ROWS, DK), F32)
    for p in reversed(range(PS)):
        send[p, :ROWS] = run.astype(BF16)
        run = decay(p) * run + recv[p, :ROWS].astype(F32)
    run = jnp.zeros((ROWS, DK), F32)
    for p in range(PS):
        send[p, ROWS:] = run.astype(BF16)
        run = decay(p) * run + recv[p, ROWS + 16 :].astype(F32)


def inner_body(q_r, g_r, v_r, key_r, beta, kd_o, local):
    low, high = low_mask()
    for n in range(BLOCKS):
        b = beta[tok_of(n)]
        grow, shrink = jnp.exp(b), jnp.exp(-b)
        q = q_r[tok_of(n)].astype(F32)
        k = key_r[tok_of(n)].astype(F32)
        q_s, k_s = q * grow, k * shrink
        for h in range(HALF):
            c = col_of(h)
            g, v = g_r[tok_of(n), c], v_r[tok_of(n), c]
            pairs = jnp.where(low, dot(g, v, NT), 0.0)
            pairs_t = jnp.where(high, dot(v, g, NT), 0.0)
            kd = shrink[:, c] * dot_ff(pairs_t, q_s[:, c])
            qd = grow[:, c] * dot_ff(pairs, k_s[:, c])
            kd_o[tok_of(n), c] = kd
            local[tok_of(n), c] = q[:, c] * qd - k[:, c] * kd


def gate_body(recv, adds, key_r, v_r, beta, q_r, g_r, kd_in, local, logit, lat, up, _,
              kd_keep, kd_give, gate_keep, gate_give, up_part, lat_part, delta, kd_o, gate_o):
    first = is_first()
    high = low_mask()[1].astype(BF16)
    back = [jnp.concatenate([recv[h * PER + i, :ROWS] for i in range(PER)], axis=0).astype(F32)
            for h in range(HALF)]
    run = [jnp.concatenate([recv[h * PER + i, ROWS:] for i in range(PER)], axis=0).astype(F32)
           for h in range(HALF)]
    grads = list(back)
    for n in reversed(range(BLOCKS)):
        b = beta[tok_of(n)]
        last = b[GROUP - 1 : GROUP]
        decay = jnp.exp(last)
        kd = jnp.concatenate(
            [dot_hl(v_r[tok_of(n), col_of(h)], grads[h]) for h in range(HALF)], axis=1
        ) * jnp.exp(last - b)
        kd_o[tok_of(n)] = (kd + kd_in[tok_of(n)]).astype(BF16)
        delta[tok_of(n)] = local[tok_of(n)] - key_r[tok_of(n)].astype(F32) * kd
        grads = [decay[:, col_of(h)] * grads[h] + adds[n, col_of(h)] for h in range(HALF)]
    for n in range(BLOCKS):
        parts, decay = added_states(key_r, v_r, beta, n)
        qd = jnp.concatenate(
            [dot_hl(g_r[tok_of(n), col_of(h)], run[h]) for h in range(HALF)], axis=1
        ) * jnp.exp(beta[tok_of(n)])
        delta[tok_of(n)] += q_r[tok_of(n)].astype(F32) * qd
        run = [decay[:, col_of(h)] * run[h] + parts[h] for h in range(HALF)]
    odd = odd_z()
    kd_lo, kd_hi = kd_o[:, :QUART], kd_o[:, QUART:]
    kd_keep[...] = pick(odd, kd_hi, kd_lo)
    kd_give[...] = pick(odd, kd_lo, kd_hi)
    beyond = jnp.concatenate(
        [jnp.sum(run[h] * back[h], axis=0, keepdims=True) for h in range(HALF)], axis=1
    )
    for n in reversed(range(BLOCKS)):
        suffix = dot_mask(high, delta[tok_of(n)]) + beyond
        beyond = suffix[:1]
        x = logit[tok_of(n)]
        gate_o[tok_of(n)] = (suffix * (1.0 / (1.0 + jnp.exp(x))) * (1.0 / 16.0)).astype(BF16)
    gate = gate_o[...]
    gate_keep[...] = pick(first, gate[:TOK], gate[TOK:])
    gate_give[...] = pick(first, gate[TOK:], gate[:TOK])
    up_half = pick(first, up[:, :WIDTH], up[:, WIDTH:])
    up_part[...] = dot(lat[...], gate, TN)
    lat_part[...] = dot(gate, up_half, NT)


SMALL = WIDTH + MODEL // 2


def weight_body(lat_a, lat_b, up_part, tok, kd_r, far, far_peer, far_kd, lat_o, send):
    first = is_first()
    latent = (lat_a[...] + lat_b[...]).astype(BF16)
    lat_o[...] = pick(first, latent[:TOK], latent[TOK:])
    half = MODEL // 2
    down = dot(latent, pick(first, tok[:, :half], tok[:, half:]), TN)
    small = jnp.concatenate([up_part[...], down], axis=1).astype(BF16)
    for p in range(PS):
        send[p, :, :SMALL] = small
    kd, kd_far = kd_r[...], far_kd[...]
    kd_a = pick(first, kd_far[:TOK], kd_far[TOK:])
    kd_b = pick(first, kd_far[TOK:], kd_far[:TOK])
    for z in range(ZS):
        cols = slice(z * 256, z * 256 + 256)
        block = dot(tok[:, cols], kd, TN)
        block = block + dot(far[:, cols], kd_a, TN) + dot(far_peer[:, cols], kd_b, TN)
        block = block.astype(BF16)
        lanes = slice(SMALL + z * QUART, SMALL + (z + 1) * QUART)
        for p in range(PS):
            send[p, :, lanes] = block[p * 16 : p * 16 + 16]


def through_body(kd, kd_far, w, w_far, keep, give):
    first = is_first()
    total = dot(kd[...], w[...], NT) + dot(kd_far[...], w_far[...], NT)
    give[...] = pick(first, total[TOK:], total[:TOK])
    keep[...] = pick(first, total[:TOK], total[TOK:])


def input_body(keep, got, lat, down, gate_m, gate_p, out, gate, flag):
    first = is_first()
    out[...] = (keep[...] + got[...] + dot(lat[...], down[...])).astype(BF16)
    gate[:, :WIDTH] = pick(first, gate_m[...], gate_p[...])
    gate[:, WIDTH:] = pick(first, gate_p[...], gate_m[...])
    flag[...] = jnp.zeros_like(flag)


PER = DK // ROWS


def plane_body(recv, send):
    total = jnp.sum(recv[...].astype(F32), axis=0).astype(BF16)
    for z in range(ZS):
        send[z, :, :SMALL] = total[:, :SMALL]
        send[z, :, SMALL:] = total[:, SMALL + z * QUART : SMALL + (z + 1) * QUART]


def total_body(recv, _, keep, give):
    first = is_first()
    parts = [recv[z].astype(F32) for z in range(ZS)]
    even, odd = sum(parts[0::2]), sum(parts[1::2])
    small = even[:, :SMALL] + odd[:, :SMALL]
    rows = jnp.concatenate([even[:, SMALL:], odd[:, SMALL:]], axis=1)
    keep[:, :SMALL] = small
    give[:, :SMALL] = small
    pad = jnp.zeros((8, WIDTH), F32)
    keep[:, SMALL:] = jnp.concatenate([pick(first, rows[:8], rows[8:]), pad], axis=0)
    give[:, SMALL:] = jnp.concatenate([pick(first, rows[8:], rows[:8]), pad], axis=0)


def out_body(mine, theirs, down_o, up_o, w_o):
    first = is_first()
    halves = (pick(first, mine[...], theirs[...]), pick(first, theirs[...], mine[...]))
    wide = MODEL // 2
    for i, a in enumerate(halves):
        up_o[:, i * WIDTH : (i + 1) * WIDTH] = a[:, :WIDTH]
        down_o[:, i * wide : (i + 1) * wide] = a[:, WIDTH:SMALL]
        w_o[:, i * WIDTH : (i + 1) * WIDTH] = a[:8, SMALL:]


def swap(a):
    return lax.ppermute(a, "c", SWAP)


def across(a):
    return lax.ppermute(a, "z", [(i, i ^ 1) for i in range(ZS)])


def a2a(a, axis):
    return lax.all_to_all(a, axis, 0, 0)


def local(inputs, queries, values, out_grad, key_weight, gate_down, gate_up, gate_bias):
    first = is_first()
    own = inputs[0]
    q, g, v = queries[0], out_grad[0], values[0]
    half_bf = shape((PAIR, WIDTH), BF16)
    half_f = shape((PAIR, WIDTH))
    packed = shape((PS, ROWS + 16, DK), BF16)
    quarter = shape((PAIR, QUART), BF16)


    w_z = key_weight.reshape(1, 8, 2, 2, QUART).transpose(0, 3, 2, 1, 4)
    w_z = jnp.broadcast_to(w_z, (ZS // 2, 2, 2, 8, QUART))
    w_z = a2a(w_z.reshape(2 * ZS, 8, QUART), ("z", "c")).reshape(ZS * 16, QUART)
    w_all = a2a(jnp.broadcast_to(w_z[None], (PS, ZS * 16, QUART)), XY)

    tok, lat, logit, beta, q, g, v, add_g, start = kernel(
        gates_body,
        (shape((PAIR, MODEL), BF16), shape((PAIR, RANK), BF16), half_f, half_f,
         half_bf, half_bf, half_bf, shape((BLOCKS, WIDTH, DK)), packed),
        "gates", BIG,
    )(own, swap(own), gate_down, gate_up, gate_bias[None], q, g, v, swap(q), swap(g), swap(v))
    far = across(own)
    far_peer = swap(far)
    tok_sems = pltpu.SemaphoreType.DMA((2,))
    keys_far, w = kernel(
        far_keys_body, (quarter, shape((MODEL, QUART), BF16)), "far_keys", FAR,
        specs=[VM, HBM, HBM, HBM], out_specs=(VM, VM),
        scratch=[pltpu.VMEM((TOK, MODEL), BF16)] * 2 + [tok_sems],
    )(w_all, far, far_peer, lat)
    keys_mine = kernel(near_keys_body, quarter, "near_keys", 16)(tok, w)
    keys, send, w = kernel(
        keys_body,
        (half_bf, shape((PS, 2 * ROWS + 16, DK), BF16), shape((MODEL, QUART), BF16)),
        "keys", 16, specs=[VM, VM, HBM, HBM, VM, HBM], out_specs=(VM, VM, HBM), alias={5: 2},
        scratch=[pltpu.VMEM((PAIR, WIDTH), F32), pltpu.VMEM((PAIR, WIDTH), BF16), tok_sems],
    )(keys_mine, across(keys_far), beta, v, start, w)
    w_far = across(w)
    recv = a2a(send, XY)
    kd_local, local_part = kernel(inner_body, (half_f, half_f), "inner", BIG)(q, g, v, keys, beta)
    recv = a2a(kernel(scan_body, shape((PS, 2 * ROWS, DK), BF16), "scan", 8)(recv), XY)
    kd_keep, kd_give, gate_m, gate_x, up_part, lat_part = kernel(
        gate_body,
        (quarter, quarter, shape((TOK, WIDTH), BF16), shape((TOK, WIDTH), BF16),
         shape((RANK, WIDTH)), shape((PAIR, RANK))),
        "gate", BIG, specs=[VM] * 12 + [HBM], out_specs=(VM,) * 6,
        scratch=[pltpu.VMEM((PAIR, WIDTH), F32)] + [pltpu.VMEM((PAIR, WIDTH), BF16)] * 2,
    )(recv, add_g, keys, v, beta, q, g, kd_local, local_part, logit, lat, gate_up, w_far)
    far_kd = across(kd_give)
    lat_own, send = kernel(
        weight_body, (shape((TOK, RANK), BF16), shape((PS, 16, SMALL + ZS * QUART), BF16)),
        "weights", BIG,
    )(lat_part, swap(lat_part), up_part, tok, kd_keep, far, far_peer, far_kd)
    send = kernel(plane_body, shape((ZS, 16, SMALL + QUART), BF16), "plane", 8)(a2a(send, XY))
    mine, other = kernel(
        through_body, (shape((TOK, MODEL)), shape((TOK, MODEL))), "through", BIG
    )(kd_keep, kd_give, w, w_far)
    input_grad, gate_grad, flag = kernel(
        input_body, (shape((TOK, MODEL), BF16), shape((TOK, 2 * WIDTH), BF16), shape((8, DK))),
        "input", 16,
    )(mine, swap(other), lat_own, gate_down, gate_m, swap(gate_x))
    end = shape((16, SMALL + WIDTH))
    keep, give = kernel(total_body, (end, end), "total", 8)(a2a(send, "z"), flag)
    down_grad, up_grad, key_weight_grad = kernel(
        out_body,
        (shape((RANK, MODEL)), shape((RANK, 2 * WIDTH)), shape((8, 2 * WIDTH))), "grads", 8,
    )(keep, swap(give))
    return (input_grad[None], gate_grad[None], key_weight_grad, down_grad, up_grad)


def solution(mesh):
    grid = Mesh(mesh.devices.reshape(8, 4, 4, 2), ("z", "x", "y", "c"))
    seq = ("x", "y", "c")
    tok = P("z", seq, None)
    row = P(("z",) + seq, None)
    return jax.shard_map(
        local,
        mesh=grid,
        in_specs=(tok, tok, tok, tok, row, P(), P(), P()),
        out_specs=(tok, tok, row, P(), P()),
        check_vma=False,
    )
```

```python
import jax
import jax.numpy as jnp
from jax import lax
from jax.experimental import pallas as pl
from jax.experimental.pallas import tpu as pltpu
from jax.sharding import Mesh, PartitionSpec as P

HEADS = 8
DK = 128
GROUP = 64
HALF = HEADS // 2
WIDTH = HALF * DK
QUART = WIDTH // 2
PER_SEQ = QUART // DK
TOK = 128
PAIR = 2 * TOK
QUAD = 2 * PAIR
BLOCKS = PAIR // GROUP
MODEL = 2048
WIDE = MODEL // 4
RANK = 16
ZS = 8
PS = 16
ROWS = HALF * DK // PS
F32 = jnp.float32
BF16 = jnp.bfloat16
XY = ("x", "y")
SWAP = ((0, 1), (1, 0))
MB = 1 << 20


def shape(dims, dtype=F32):
    return jax.ShapeDtypeStruct(dims, dtype)


BIG = 56


VM = pl.BlockSpec(memory_space=pltpu.VMEM)
HBM = pl.BlockSpec(memory_space=pltpu.HBM)


def kernel(body, outs, name, limit, scratch=(), specs=None, out_specs=None, alias=None):
    extra = {} if specs is None else {"in_specs": specs, "out_specs": out_specs}
    if alias:
        extra["input_output_aliases"] = alias
    return pl.pallas_call(
        body,
        out_shape=outs,
        name=name,
        scratch_shapes=scratch,
        compiler_params=pltpu.CompilerParams(vmem_limit_bytes=limit * MB),
        **extra,
    )


def split(a):
    hi = a.astype(BF16)
    return hi, (a - hi.astype(F32)).astype(BF16)


def dot(a, b, dims=((1,), (0,))):
    return lax.dot_general(a, b, (dims, ((), ())), preferred_element_type=F32)


NT = ((1,), (1,))
TN = ((0,), (0,))


def dot_hl(a, b, dims=((1,), (0,))):
    hi, lo = split(b)
    return dot(a, hi, dims) + dot(a, lo, dims)


def dot_ff(a, b, dims=((1,), (0,))):
    ah, al = split(a)
    bh, bl = split(b)
    return dot(ah, bh, dims) + dot(ah, bl, dims) + dot(al, bh, dims)


def dot_mask(mask, b):
    hi, lo = split(b)
    rest = (b - hi.astype(F32) - lo.astype(F32)).astype(BF16)
    return dot(mask, hi) + dot(mask, lo) + dot(mask, rest)


def is_first():
    return lax.axis_index("c") == 0


def pick(first, a, b):
    return jnp.where(first, a, b)


def low_mask():
    rows = lax.broadcasted_iota(jnp.int32, (GROUP, GROUP), 0)
    cols = lax.broadcasted_iota(jnp.int32, (GROUP, GROUP), 1)
    return rows >= cols, rows <= cols


def tok_of(n):
    return slice(n * GROUP, (n + 1) * GROUP)


def col_of(h):
    return slice(h * DK, (h + 1) * DK)


def span_of(beta, n):
    return beta[(n + 1) * GROUP - 1 : (n + 1) * GROUP]


def odd_z():
    return lax.rem(lax.axis_index("z"), 2) == 1


def quarter_of(ref, core, odd):
    lo = pick(odd, ref[:, QUART : 2 * QUART], ref[:, :QUART])
    hi = pick(odd, ref[:, 3 * QUART :], ref[:, 2 * QUART : 3 * QUART])
    return pick(core, lo, hi)


def prep_body(q, g, v, keep, to_c, to_z, to_cz):
    first, odd = is_first(), odd_z()
    other, even = jnp.logical_not(first), jnp.logical_not(odd)
    for i, ref in enumerate((q, g, v)):
        rows = slice(i * TOK, (i + 1) * TOK)
        keep[rows] = quarter_of(ref, first, odd)
        to_c[rows] = quarter_of(ref, other, odd)
        to_z[rows] = quarter_of(ref, first, even)
        to_cz[rows] = quarter_of(ref, other, even)


def rows_of(seq, n):
    at = seq * PAIR + n * GROUP
    return slice(at, at + GROUP)


def state_of(seq, h):
    return seq * PER_SEQ + h


def gates_body(own, peer, far, far_peer, down, up, bias, tok, lat, logit, beta):
    first, odd = is_first(), odd_z()
    tok[:TOK] = pick(first, own[...], peer[...])
    tok[TOK:PAIR] = pick(first, peer[...], own[...])
    tok[PAIR : PAIR + TOK] = pick(first, far[...], far_peer[...])
    tok[PAIR + TOK :] = pick(first, far_peer[...], far[...])
    latent = dot(tok[...], down[...], NT).astype(BF16)
    lat[...] = latent
    x = dot(latent, quarter_of(up, first, odd)) + quarter_of(bias, first, odd)
    logit[...] = x
    gamma = (jnp.minimum(x, 0.0) - jnp.log1p(jnp.exp(-jnp.abs(x)))) * (1.0 / 16.0)
    lower = low_mask()[0].astype(BF16)
    for n in range(QUAD // GROUP):
        beta[tok_of(n)] = dot_mask(lower, gamma[tok_of(n)])


def start_body(mine, from_c, from_z, from_cz, beta, q_o, g_o, v_o, adds, start):
    first = is_first()
    for i, out in enumerate((q_o, g_o, v_o)):
        rows = slice(i * TOK, (i + 1) * TOK)
        a, b, c, d = mine[rows], from_c[rows], from_z[rows], from_cz[rows]
        out[:TOK] = pick(first, a, b)
        out[TOK:PAIR] = pick(first, b, a)
        out[PAIR : PAIR + TOK] = pick(first, c, d)
        out[PAIR + TOK :] = pick(first, d, c)
    run = [jnp.zeros((DK, DK), F32)] * HALF
    decays = []
    for seq in range(2):
        total = jnp.zeros((1, QUART), F32)
        for n in reversed(range(BLOCKS)):
            r = rows_of(seq, n)
            b = beta[r]
            last = b[GROUP - 1 : GROUP]
            total = total + last
            decay = jnp.exp(last)
            scaled = q_o[r].astype(F32) * jnp.exp(b)
            grad = g_o[r]
            for h in range(PER_SEQ):
                s = state_of(seq, h)
                part = dot_hl(grad[:, col_of(h)], scaled[:, col_of(h)], TN)
                adds[n, col_of(s)] = part
                run[s] = decay[:, col_of(h)] * run[s] + part
        decays.append(jnp.exp(total))
    for p in range(PS):
        s, at = p // PER, (p % PER) * ROWS
        row = decays[s // PER_SEQ][:, col_of(s % PER_SEQ)]
        start[p, :ROWS] = run[s][at : at + ROWS].astype(BF16)
        top = row.astype(BF16).astype(F32)
        start[p, ROWS:] = jnp.concatenate(
            [jnp.broadcast_to(top, (8, DK)), jnp.broadcast_to(row - top, (8, DK))], axis=0
        ).astype(BF16)


def added_states(key, v, beta, seq, n):
    r = rows_of(seq, n)
    b = beta[r]
    last = b[GROUP - 1 : GROUP]
    tail = key[r].astype(F32) * jnp.exp(last - b)
    vals = v[r]
    return [dot_hl(vals[:, col_of(h)], tail[:, col_of(h)], TN) for h in range(PER_SEQ)], jnp.exp(last)


def load(pairs, sems):
    copies = [pltpu.make_async_copy(a, b, sems.at[i]) for i, (a, b) in enumerate(pairs)]
    for copy in copies:
        copy.start()
    return copies


def unpack(recv, w):
    for p in range(PS):
        for z in range(ZS):
            w[z * 256 + p * 16 : z * 256 + p * 16 + 16] = recv[p, z * 16 : z * 16 + 16]


def keys_body(recv_h, tok_h, beta_h, v_h, start_h, key_o, send, w_o,
              recv, tok, beta, v, start, w, sems):
    copies = load(
        ((recv_h, recv), (tok_h, tok), (beta_h, beta), (v_h, v), (start_h, start)), sems
    )
    copies[0].wait()
    unpack(recv, w)
    for copy in copies[1:]:
        copy.wait()
    key_o[...] = dot(tok[...], w[...]).astype(BF16)
    run = [jnp.zeros((DK, DK), F32)] * HALF
    for seq in range(2):
        for n in range(BLOCKS):
            parts, decay = added_states(key_o, v, beta, seq, n)
            for h in range(PER_SEQ):
                s = state_of(seq, h)
                run[s] = decay[:, col_of(h)] * run[s] + parts[h]
    for p in range(PS):
        s, at = p // PER, (p % PER) * ROWS
        send[p, : ROWS + 16] = start[p]
        send[p, ROWS + 16 :] = run[s][at : at + ROWS].astype(BF16)


def scan_body(recv, send):
    def decay(p):
        rows = recv[p, ROWS : ROWS + 16].astype(F32)
        return rows[:1] + rows[8:9]

    run = jnp.zeros((ROWS, DK), F32)
    for p in reversed(range(PS)):
        send[p, :ROWS] = run.astype(BF16)
        run = decay(p) * run + recv[p, :ROWS].astype(F32)
    run = jnp.zeros((ROWS, DK), F32)
    for p in range(PS):
        send[p, ROWS:] = run.astype(BF16)
        run = decay(p) * run + recv[p, ROWS + 16 :].astype(F32)


def inner_body(q_r, g_r, v_r, key_r, beta, kd_o, local):
    low, high = low_mask()
    for n in range(QUAD // GROUP):
        r = tok_of(n)
        b = beta[r]
        grow, shrink = jnp.exp(b), jnp.exp(-b)
        q = q_r[r].astype(F32)
        k = key_r[r].astype(F32)
        q_s, k_s = q * grow, k * shrink
        for h in range(PER_SEQ):
            c = col_of(h)
            g, v = g_r[r, c], v_r[r, c]
            pairs = jnp.where(low, dot(g, v, NT), 0.0)
            pairs_t = jnp.where(high, dot(v, g, NT), 0.0)
            kd = shrink[:, c] * dot_ff(pairs_t, q_s[:, c])
            qd = grow[:, c] * dot_ff(pairs, k_s[:, c])
            kd_o[r, c] = kd
            local[r, c] = q[:, c] * qd - k[:, c] * kd


def chip_rows(recv, at):
    return [
        jnp.concatenate([recv[s * PER + i, at : at + ROWS] for i in range(PER)], axis=0).astype(F32)
        for s in range(HALF)
    ]


def gate_body(recv, adds, key_r, v_r, beta, q_r, g_r, kd_in, local, logit, lat, up, _,
              kd_o, gate_o, up_part, lat_part, delta):
    first, odd = is_first(), odd_z()
    high = low_mask()[1].astype(BF16)
    back, run = chip_rows(recv, 0), chip_rows(recv, ROWS)
    grads = list(back)
    for seq in range(2):
        states = [state_of(seq, h) for h in range(PER_SEQ)]
        for n in reversed(range(BLOCKS)):
            r = rows_of(seq, n)
            b = beta[r]
            last = b[GROUP - 1 : GROUP]
            decay = jnp.exp(last)
            kd = jnp.concatenate(
                [dot_hl(v_r[r, col_of(h)], grads[s]) for h, s in enumerate(states)], axis=1
            ) * jnp.exp(last - b)
            kd_o[r] = (kd + kd_in[r]).astype(BF16)
            delta[r] = local[r] - key_r[r].astype(F32) * kd
            for h, s in enumerate(states):
                grads[s] = decay[:, col_of(h)] * grads[s] + adds[n, col_of(s)]
        for n in range(BLOCKS):
            r = rows_of(seq, n)
            parts, decay = added_states(key_r, v_r, beta, seq, n)
            qd = jnp.concatenate(
                [dot_hl(g_r[r, col_of(h)], run[s]) for h, s in enumerate(states)], axis=1
            ) * jnp.exp(beta[r])
            delta[r] += q_r[r].astype(F32) * qd
            for h, s in enumerate(states):
                run[s] = decay[:, col_of(h)] * run[s] + parts[h]
        beyond = jnp.concatenate(
            [jnp.sum(run[s] * back[s], axis=0, keepdims=True) for s in states], axis=1
        )
        for n in reversed(range(BLOCKS)):
            r = rows_of(seq, n)
            suffix = dot_mask(high, delta[r]) + beyond
            beyond = suffix[:1]
            x = logit[r]
            gate_o[r] = (suffix * (1.0 / (1.0 + jnp.exp(x))) * (1.0 / 16.0)).astype(BF16)
    gate = gate_o[...]
    up_part[...] = dot(lat[...], gate, TN)
    lat_part[...] = dot(quarter_of(up, first, odd), gate, NT)


SMALL = QUART + WIDE


def weight_body(lat_a, lat_c, lat_z, lat_cz, up_part, tok, kd_r, lat_o, send):
    first, odd = is_first(), odd_z()
    near = lat_a[...] + lat_c[...]
    far = lat_z[...] + lat_cz[...]
    latent = jnp.concatenate(
        [near[:, :PAIR] + far[:, PAIR:], near[:, PAIR:] + far[:, :PAIR]], axis=1
    ).astype(BF16)
    lat_o[...] = pick(first, latent[:, :TOK], latent[:, TOK:PAIR])
    lo = pick(odd, tok[:, WIDE : 2 * WIDE], tok[:, :WIDE])
    hi = pick(odd, tok[:, 3 * WIDE :], tok[:, 2 * WIDE : 3 * WIDE])
    down = dot(latent, pick(first, lo, hi))
    small = jnp.concatenate([up_part[...], down], axis=1).astype(BF16)
    for p in range(PS):
        send[p, :, :SMALL] = small
    kd = kd_r[...]
    for z in range(ZS):
        block = dot(tok[:, z * 256 : z * 256 + 256], kd, TN).astype(BF16)
        lanes = slice(SMALL + z * QUART, SMALL + (z + 1) * QUART)
        for p in range(PS):
            send[p, :, lanes] = block[p * 16 : p * 16 + 16]


def share_body(gate, keep, to_c, to_z, to_cz):
    first = is_first()
    keep[...] = pick(first, gate[:TOK], gate[TOK:PAIR])
    to_c[...] = pick(first, gate[TOK:PAIR], gate[:TOK])
    to_z[...] = pick(first, gate[PAIR : PAIR + TOK], gate[PAIR + TOK :])
    to_cz[...] = pick(first, gate[PAIR + TOK :], gate[PAIR : PAIR + TOK])


def through_body(kd, kd_far, w_all, far_all, keep, give, w, w_far):
    first = is_first()
    unpack(w_all, w)
    unpack(far_all, w_far)
    total = dot(kd[...], w[...], NT) + dot(kd_far[...], w_far[...], NT)
    give[...] = pick(first, total[TOK:], total[:TOK])
    keep[...] = pick(first, total[:TOK], total[TOK:])


def input_body(keep, got, lat, down, gate_m, gate_c, gate_z, gate_cz, out, gate, flag):
    first, odd = is_first(), odd_z()
    out[...] = (keep[...] + got[...] + dot(lat[...], down[...], TN)).astype(BF16)
    mine = jnp.concatenate(
        [pick(odd, gate_z[...], gate_m[...]), pick(odd, gate_m[...], gate_z[...])], axis=1
    )
    theirs = jnp.concatenate(
        [pick(odd, gate_cz[...], gate_c[...]), pick(odd, gate_c[...], gate_cz[...])], axis=1
    )
    gate[:, :WIDTH] = pick(first, mine, theirs)
    gate[:, WIDTH:] = pick(first, theirs, mine)
    flag[...] = jnp.zeros_like(flag)


PER = DK // ROWS


def plane_body(recv, _, send):
    total = jnp.sum(recv[...].astype(F32), axis=0).astype(BF16)
    for z in range(ZS):
        send[z, :, :SMALL] = total[:, :SMALL]
        send[z, :, SMALL:] = total[:, SMALL + z * QUART : SMALL + (z + 1) * QUART]


HALVES = WIDTH + MODEL // 2


def total_body(recv, keep, give):
    first = is_first()
    parts = [recv[z].astype(F32) for z in range(ZS)]
    even, odd = sum(parts[0::2]), sum(parts[1::2])
    small = jnp.concatenate(
        [even[:, :QUART], odd[:, :QUART], even[:, QUART:SMALL], odd[:, QUART:SMALL]], axis=1
    )
    rows = jnp.concatenate([even[:, SMALL:], odd[:, SMALL:]], axis=1)
    keep[:, :HALVES] = small
    give[:, :HALVES] = small
    pad = jnp.zeros((8, WIDTH), F32)
    keep[:, HALVES:] = jnp.concatenate([pick(first, rows[:8], rows[8:]), pad], axis=0)
    give[:, HALVES:] = jnp.concatenate([pick(first, rows[8:], rows[:8]), pad], axis=0)


def out_body(mine, theirs, down_o, up_o, w_o):
    first = is_first()
    halves = (pick(first, mine[...], theirs[...]), pick(first, theirs[...], mine[...]))
    wide = MODEL // 2
    for i, a in enumerate(halves):
        up_o[:, i * WIDTH : (i + 1) * WIDTH] = a[:, :WIDTH]
        down_o[:, i * wide : (i + 1) * wide] = a[:, WIDTH:HALVES]
        w_o[:, i * WIDTH : (i + 1) * WIDTH] = a[:8, HALVES:]


def swap(a):
    return lax.ppermute(a, "c", SWAP)


def cross(a):
    pairs = [(z * 2 + c, (z ^ 1) * 2 + (1 - c)) for z in range(ZS) for c in range(2)]
    return lax.ppermute(a, ("z", "c"), pairs)


def across(a):
    return lax.ppermute(a, "z", [(i, i ^ 1) for i in range(ZS)])


def a2a(a, axis):
    return lax.all_to_all(a, axis, 0, 0)


def local(inputs, queries, values, out_grad, key_weight, gate_down, gate_up, gate_bias):
    own = inputs[0]
    w_z = key_weight.reshape(1, 8, 2, 2, QUART).transpose(0, 3, 2, 1, 4)
    w_z = jnp.broadcast_to(w_z, (ZS // 2, 2, 2, 8, QUART))
    w_z = a2a(w_z.reshape(2 * ZS, 8, QUART), ("z", "c")).reshape(ZS * 16, QUART)
    w_all = a2a(jnp.broadcast_to(w_z[None], (PS, ZS * 16, QUART)), XY)

    third = shape((3 * TOK, QUART), BF16)
    mine, to_c, to_z, to_cz = kernel(prep_body, (third,) * 4, "prep", BIG)(
        queries[0], out_grad[0], values[0]
    )
    far = across(own)
    quad_bf = shape((QUAD, QUART), BF16)
    quad_f = shape((QUAD, QUART))
    tok, lat, logit, beta = kernel(
        gates_body,
        (shape((QUAD, MODEL), BF16), shape((QUAD, RANK), BF16), quad_f, quad_f), "gates", BIG,
    )(own, swap(own), far, swap(far), gate_down, gate_up, gate_bias[None])
    q, g, v, add_g, start = kernel(
        start_body,
        (quad_bf, quad_bf, quad_bf, shape((BLOCKS, WIDTH, DK)),
         shape((PS, ROWS + 16, DK), BF16)),
        "start", BIG,
    )(mine, swap(to_c), across(to_z), cross(to_cz), beta)
    keys, send, w_all = kernel(
        keys_body,
        (quad_bf, shape((PS, 2 * ROWS + 16, DK), BF16), shape((PS, ZS * 16, QUART), BF16)),
        "keys", BIG, specs=[HBM] * 5, out_specs=(VM, VM, HBM), alias={0: 2},
        scratch=[pltpu.VMEM((PS, ZS * 16, QUART), BF16), pltpu.VMEM((QUAD, MODEL), BF16),
                 pltpu.VMEM((QUAD, QUART), F32), pltpu.VMEM((QUAD, QUART), BF16),
                 pltpu.VMEM((PS, ROWS + 16, DK), BF16), pltpu.VMEM((MODEL, QUART), BF16),
                 pltpu.SemaphoreType.DMA((5,))],
    )(w_all, tok, beta, v, start)
    w_far = across(w_all)
    recv = a2a(send, XY)
    kd_local, local_part = kernel(inner_body, (quad_f, quad_f), "inner", BIG)(q, g, v, keys, beta)
    recv = a2a(kernel(scan_body, shape((PS, 2 * ROWS, DK), BF16), "scan", 8)(recv), XY)
    kd, gate, up_part, lat_part = kernel(
        gate_body,
        (quad_bf, quad_bf, shape((RANK, QUART)), shape((RANK, QUAD))),
        "gate", BIG, specs=[VM] * 12 + [HBM], out_specs=(VM,) * 4,
        scratch=[pltpu.VMEM((QUAD, QUART), F32)],
    )(recv, add_g, keys, v, beta, q, g, kd_local, local_part, logit, lat, gate_up, w_far)
    lat_own, send = kernel(
        weight_body, (shape((RANK, TOK), BF16), shape((PS, 16, SMALL + ZS * QUART), BF16)),
        "weights", BIG,
    )(lat_part, swap(lat_part), across(lat_part), cross(lat_part), up_part, tok, kd)
    keep, give = kernel(
        through_body, (shape((TOK, MODEL)), shape((TOK, MODEL))), "through", BIG,
        scratch=[pltpu.VMEM((MODEL, QUART), BF16)] * 2,
    )(kd[:PAIR], across(kd[PAIR:]), w_all, w_far)
    piece = shape((TOK, QUART), BF16)
    gate_m, gate_c, gate_z, gate_cz = kernel(share_body, (piece,) * 4, "share", 8)(gate)
    input_grad, gate_grad, flag = kernel(
        input_body, (shape((TOK, MODEL), BF16), shape((TOK, 2 * WIDTH), BF16), shape((8, DK))),
        "input", 16,
    )(keep, swap(give), lat_own, gate_down, gate_m, swap(gate_c), across(gate_z), cross(gate_cz))
    send = kernel(plane_body, shape((ZS, 16, SMALL + QUART), BF16), "plane", 8)(
        a2a(send, XY), flag
    )
    end = shape((16, HALVES + WIDTH))
    keep, give = kernel(total_body, (end, end), "total", 8)(a2a(send, "z"))
    down_grad, up_grad, key_weight_grad = kernel(
        out_body,
        (shape((RANK, MODEL)), shape((RANK, 2 * WIDTH)), shape((8, 2 * WIDTH))), "grads", 8,
    )(keep, swap(give))
    return (input_grad[None], gate_grad[None], key_weight_grad, down_grad, up_grad)


def solution(mesh):
    grid = Mesh(mesh.devices.reshape(8, 4, 4, 2), ("z", "x", "y", "c"))
    seq = ("x", "y", "c")
    tok = P("z", seq, None)
    row = P(("z",) + seq, None)
    return jax.shard_map(
        local,
        mesh=grid,
        in_specs=(tok, tok, tok, tok, row, P(), P(), P()),
        out_specs=(tok, tok, row, P(), P()),
        check_vma=False,
    )
```

```python
import jax
import jax.numpy as jnp
from jax import lax
from jax.experimental import pallas as pl
from jax.experimental.pallas import tpu as pltpu
from jax.sharding import Mesh, PartitionSpec as P

HEADS = 8
DK = 128
GROUP = 64
HALF = HEADS // 2
WIDTH = HALF * DK
QUART = WIDTH // 2
PER_SEQ = QUART // DK
TOK = 128
PAIR = 2 * TOK
QUAD = 2 * PAIR
BLOCKS = PAIR // GROUP
MODEL = 2048
WIDE = MODEL // 4
RANK = 16
ZS = 8
PS = 16
ROWS = HALF * DK // PS
F32 = jnp.float32
BF16 = jnp.bfloat16
XY = ("x", "y")
SWAP = ((0, 1), (1, 0))
MB = 1 << 20


def shape(dims, dtype=F32):
    return jax.ShapeDtypeStruct(dims, dtype)


BIG = 56


VM = pl.BlockSpec(memory_space=pltpu.VMEM)
HBM = pl.BlockSpec(memory_space=pltpu.HBM)


def kernel(body, outs, name, limit, scratch=(), specs=None, out_specs=None, alias=None):
    extra = {} if specs is None else {"in_specs": specs, "out_specs": out_specs}
    if alias:
        extra["input_output_aliases"] = alias
    return pl.pallas_call(
        body,
        out_shape=outs,
        name=name,
        scratch_shapes=scratch,
        compiler_params=pltpu.CompilerParams(vmem_limit_bytes=limit * MB),
        **extra,
    )


def split(a):
    hi = a.astype(BF16)
    return hi, (a - hi.astype(F32)).astype(BF16)


def dot(a, b, dims=((1,), (0,))):
    return lax.dot_general(a, b, (dims, ((), ())), preferred_element_type=F32)


NT = ((1,), (1,))
TN = ((0,), (0,))


def dot_hl(a, b, dims=((1,), (0,))):
    hi, lo = split(b)
    return dot(a, hi, dims) + dot(a, lo, dims)


def dot_ff(a, b, dims=((1,), (0,))):
    ah, al = split(a)
    bh, bl = split(b)
    return dot(ah, bh, dims) + dot(ah, bl, dims) + dot(al, bh, dims)


def dot_mask(mask, b):
    hi, lo = split(b)
    rest = (b - hi.astype(F32) - lo.astype(F32)).astype(BF16)
    return dot(mask, hi) + dot(mask, lo) + dot(mask, rest)


def is_first():
    return lax.axis_index("c") == 0


def pick(first, a, b):
    return jnp.where(first, a, b)


def low_mask():
    rows = lax.broadcasted_iota(jnp.int32, (GROUP, GROUP), 0)
    cols = lax.broadcasted_iota(jnp.int32, (GROUP, GROUP), 1)
    return rows >= cols, rows <= cols


def tok_of(n):
    return slice(n * GROUP, (n + 1) * GROUP)


def col_of(h):
    return slice(h * DK, (h + 1) * DK)


def span_of(beta, n):
    return beta[(n + 1) * GROUP - 1 : (n + 1) * GROUP]


def odd_z():
    return lax.rem(lax.axis_index("z"), 2) == 1


def quarter_of(ref, core, odd):
    lo = pick(odd, ref[:, QUART : 2 * QUART], ref[:, :QUART])
    hi = pick(odd, ref[:, 3 * QUART :], ref[:, 2 * QUART : 3 * QUART])
    return pick(core, lo, hi)


def prep_body(q, g, v, keep, to_c, to_z, to_cz):
    first, odd = is_first(), odd_z()
    other, even = jnp.logical_not(first), jnp.logical_not(odd)
    for i, ref in enumerate((q, g, v)):
        rows = slice(i * TOK, (i + 1) * TOK)
        keep[rows] = quarter_of(ref, first, odd)
        to_c[rows] = quarter_of(ref, other, odd)
        to_z[rows] = quarter_of(ref, first, even)
        to_cz[rows] = quarter_of(ref, other, even)


def rows_of(seq, n):
    at = seq * PAIR + n * GROUP
    return slice(at, at + GROUP)


def state_of(seq, h):
    return seq * PER_SEQ + h


def gates_body(own, peer, far, far_peer, down, up, bias, tok, lat, logit, beta):
    first, odd = is_first(), odd_z()
    tok[:TOK] = pick(first, own[...], peer[...])
    tok[TOK:PAIR] = pick(first, peer[...], own[...])
    tok[PAIR : PAIR + TOK] = pick(first, far[...], far_peer[...])
    tok[PAIR + TOK :] = pick(first, far_peer[...], far[...])
    latent = dot(tok[...], down[...], NT).astype(BF16)
    lat[...] = latent
    x = dot(latent, quarter_of(up, first, odd)) + quarter_of(bias, first, odd)
    logit[...] = x
    gamma = (jnp.minimum(x, 0.0) - jnp.log1p(jnp.exp(-jnp.abs(x)))) * (1.0 / 16.0)
    lower = low_mask()[0].astype(BF16)
    for n in range(QUAD // GROUP):
        beta[tok_of(n)] = dot_mask(lower, gamma[tok_of(n)])


def assemble(out, a, b, c, d):
    first = is_first()
    out[:TOK] = pick(first, a, b)
    out[TOK:PAIR] = pick(first, b, a)
    out[PAIR : PAIR + TOK] = pick(first, c, d)
    out[PAIR + TOK :] = pick(first, d, c)


def added_grads(q, g, beta, seq, n):
    r = rows_of(seq, n)
    b = beta[r]
    scaled = q[r].astype(F32) * jnp.exp(b)
    grad = g[r]
    return [dot_hl(grad[:, col_of(h)], scaled[:, col_of(h)], TN) for h in range(PER_SEQ)], b[-1:]


def start_states(q, g, beta, send):
    run = [jnp.zeros((DK, DK), F32)] * HALF
    decays = []
    for seq in range(2):
        total = jnp.zeros((1, QUART), F32)
        for n in reversed(range(BLOCKS)):
            parts, last = added_grads(q, g, beta, seq, n)
            total = total + last
            decay = jnp.exp(last)
            for h in range(PER_SEQ):
                s = state_of(seq, h)
                run[s] = decay[:, col_of(h)] * run[s] + parts[h]
        decays.append(jnp.exp(total))
    for p in range(PS):
        s, at = p // PER, (p % PER) * ROWS
        row = decays[s // PER_SEQ][:, col_of(s % PER_SEQ)]
        send[p, :ROWS] = run[s][at : at + ROWS].astype(BF16)
        top = row.astype(BF16).astype(F32)
        send[p, ROWS : ROWS + 16] = jnp.concatenate(
            [jnp.broadcast_to(top, (8, DK)), jnp.broadcast_to(row - top, (8, DK))], axis=0
        ).astype(BF16)


def added_states(key, v, beta, seq, n):
    r = rows_of(seq, n)
    b = beta[r]
    last = b[GROUP - 1 : GROUP]
    tail = key[r].astype(F32) * jnp.exp(last - b)
    vals = v[r]
    return [dot_hl(vals[:, col_of(h)], tail[:, col_of(h)], TN) for h in range(PER_SEQ)], jnp.exp(last)


def load(pairs, sems):
    copies = [pltpu.make_async_copy(a, b, sems.at[i]) for i, (a, b) in enumerate(pairs)]
    for copy in copies:
        copy.start()
    return copies


def unpack(recv, w):
    for p in range(PS):
        for z in range(ZS):
            w[z * 256 + p * 16 : z * 256 + p * 16 + 16] = recv[p, z * 16 : z * 16 + 16]


def keys_body(recv_h, tok_h, beta_h, mine, from_c, from_z, from_cz, key_o, send, w_o,
              recv, tok, beta, parts, q, g, v, w, sems):
    copies = load(
        [(beta_h, beta)]
        + [(a, parts.at[i]) for i, a in enumerate((mine, from_c, from_z, from_cz))]
        + [(recv_h, recv), (tok_h, tok)],
        sems,
    )
    for copy in copies[:5]:
        copy.wait()
    for i, out in enumerate((q, g, v)):
        assemble(out, *(parts[j, i * TOK : (i + 1) * TOK] for j in range(4)))
    start_states(q, g, beta, send)
    copies[5].wait()
    unpack(recv, w)
    copies[6].wait()
    key_o[...] = dot(tok[...], w[...]).astype(BF16)
    run = [jnp.zeros((DK, DK), F32)] * HALF
    for seq in range(2):
        for n in range(BLOCKS):
            parts, decay = added_states(key_o, v, beta, seq, n)
            for h in range(PER_SEQ):
                s = state_of(seq, h)
                run[s] = decay[:, col_of(h)] * run[s] + parts[h]
    for p in range(PS):
        s, at = p // PER, (p % PER) * ROWS
        send[p, ROWS + 16 :] = run[s][at : at + ROWS].astype(BF16)


def scan_body(recv, send):
    def decay(p):
        rows = recv[p, ROWS : ROWS + 16].astype(F32)
        return rows[:1] + rows[8:9]

    run = jnp.zeros((ROWS, DK), F32)
    for p in reversed(range(PS)):
        send[p, :ROWS] = run.astype(BF16)
        run = decay(p) * run + recv[p, :ROWS].astype(F32)
    run = jnp.zeros((ROWS, DK), F32)
    for p in range(PS):
        send[p, ROWS:] = run.astype(BF16)
        run = decay(p) * run + recv[p, ROWS + 16 :].astype(F32)


def inner_body(mine, from_c, from_z, from_cz, key_r, beta, kd_o, local, q_r, g_r, v_r, adds):
    low, high = low_mask()
    for i, out in enumerate((q_r, g_r, v_r)):
        rows = slice(i * TOK, (i + 1) * TOK)
        assemble(out, mine[rows], from_c[rows], from_z[rows], from_cz[rows])
    for seq in range(2):
        for n in range(BLOCKS):
            parts, _ = added_grads(q_r, g_r, beta, seq, n)
            for h in range(PER_SEQ):
                adds[n, col_of(state_of(seq, h))] = parts[h]
    for n in range(QUAD // GROUP):
        r = tok_of(n)
        b = beta[r]
        grow, shrink = jnp.exp(b), jnp.exp(-b)
        q = q_r[r].astype(F32)
        k = key_r[r].astype(F32)
        q_s, k_s = q * grow, k * shrink
        for h in range(PER_SEQ):
            c = col_of(h)
            g, v = g_r[r, c], v_r[r, c]
            pairs = jnp.where(low, dot(g, v, NT), 0.0)
            pairs_t = jnp.where(high, dot(v, g, NT), 0.0)
            kd = shrink[:, c] * dot_ff(pairs_t, q_s[:, c])
            qd = grow[:, c] * dot_ff(pairs, k_s[:, c])
            kd_o[r, c] = kd
            local[r, c] = q[:, c] * qd - k[:, c] * kd


def chip_rows(recv, at):
    return [
        jnp.concatenate([recv[s * PER + i, at : at + ROWS] for i in range(PER)], axis=0).astype(F32)
        for s in range(HALF)
    ]


def gate_body(recv, adds, key_r, v_r, beta, q_r, g_r, kd_in, local, logit, lat, up, _,
              kd_o, gate_o, up_part, lat_part, delta):
    first, odd = is_first(), odd_z()
    high = low_mask()[1].astype(BF16)
    back, run = chip_rows(recv, 0), chip_rows(recv, ROWS)
    grads = list(back)
    for seq in range(2):
        states = [state_of(seq, h) for h in range(PER_SEQ)]
        for n in reversed(range(BLOCKS)):
            r = rows_of(seq, n)
            b = beta[r]
            last = b[GROUP - 1 : GROUP]
            decay = jnp.exp(last)
            kd = jnp.concatenate(
                [dot_hl(v_r[r, col_of(h)], grads[s]) for h, s in enumerate(states)], axis=1
            ) * jnp.exp(last - b)
            kd_o[r] = (kd + kd_in[r]).astype(BF16)
            delta[r] = local[r] - key_r[r].astype(F32) * kd
            for h, s in enumerate(states):
                grads[s] = decay[:, col_of(h)] * grads[s] + adds[n, col_of(s)]
        for n in range(BLOCKS):
            r = rows_of(seq, n)
            parts, decay = added_states(key_r, v_r, beta, seq, n)
            qd = jnp.concatenate(
                [dot_hl(g_r[r, col_of(h)], run[s]) for h, s in enumerate(states)], axis=1
            ) * jnp.exp(beta[r])
            delta[r] += q_r[r].astype(F32) * qd
            for h, s in enumerate(states):
                run[s] = decay[:, col_of(h)] * run[s] + parts[h]
        beyond = jnp.concatenate(
            [jnp.sum(run[s] * back[s], axis=0, keepdims=True) for s in states], axis=1
        )
        for n in reversed(range(BLOCKS)):
            r = rows_of(seq, n)
            suffix = dot_mask(high, delta[r]) + beyond
            beyond = suffix[:1]
            x = logit[r]
            gate_o[r] = (suffix * (1.0 / (1.0 + jnp.exp(x))) * (1.0 / 16.0)).astype(BF16)
    gate = gate_o[...]
    up_part[...] = dot(lat[...], gate, TN)
    lat_part[...] = dot(quarter_of(up, first, odd), gate, NT)


SMALL = QUART + WIDE


def weight_body(lat_a, lat_c, lat_z, lat_cz, up_part, tok, kd_r, lat_o, send):
    first, odd = is_first(), odd_z()
    near = lat_a[...] + lat_c[...]
    far = lat_z[...] + lat_cz[...]
    latent = jnp.concatenate(
        [near[:, :PAIR] + far[:, PAIR:], near[:, PAIR:] + far[:, :PAIR]], axis=1
    ).astype(BF16)
    lat_o[...] = pick(first, latent[:, :TOK], latent[:, TOK:PAIR])
    lo = pick(odd, tok[:, WIDE : 2 * WIDE], tok[:, :WIDE])
    hi = pick(odd, tok[:, 3 * WIDE :], tok[:, 2 * WIDE : 3 * WIDE])
    down = dot(latent, pick(first, lo, hi))
    small = jnp.concatenate([up_part[...], down], axis=1).astype(BF16)
    for p in range(PS):
        send[p, :, :SMALL] = small
    kd = kd_r[...]
    for z in range(ZS):
        block = dot(tok[:, z * 256 : z * 256 + 256], kd, TN).astype(BF16)
        lanes = slice(SMALL + z * QUART, SMALL + (z + 1) * QUART)
        for p in range(PS):
            send[p, :, lanes] = block[p * 16 : p * 16 + 16]


def share_body(gate, keep, to_c, to_z, to_cz):
    first = is_first()
    keep[...] = pick(first, gate[:TOK], gate[TOK:PAIR])
    to_c[...] = pick(first, gate[TOK:PAIR], gate[:TOK])
    to_z[...] = pick(first, gate[PAIR : PAIR + TOK], gate[PAIR + TOK :])
    to_cz[...] = pick(first, gate[PAIR + TOK :], gate[PAIR : PAIR + TOK])


def through_body(kd, kd_far, w_all, far_all, keep, give, w, w_far):
    first = is_first()
    unpack(w_all, w)
    unpack(far_all, w_far)
    total = dot(kd[...], w[...], NT) + dot(kd_far[...], w_far[...], NT)
    give[...] = pick(first, total[TOK:], total[:TOK])
    keep[...] = pick(first, total[:TOK], total[TOK:])


def input_body(keep, got, lat, down, gate_m, gate_c, gate_z, gate_cz, out, gate, flag):
    first, odd = is_first(), odd_z()
    out[...] = (keep[...] + got[...] + dot(lat[...], down[...], TN)).astype(BF16)
    mine = jnp.concatenate(
        [pick(odd, gate_z[...], gate_m[...]), pick(odd, gate_m[...], gate_z[...])], axis=1
    )
    theirs = jnp.concatenate(
        [pick(odd, gate_cz[...], gate_c[...]), pick(odd, gate_c[...], gate_cz[...])], axis=1
    )
    gate[:, :WIDTH] = pick(first, mine, theirs)
    gate[:, WIDTH:] = pick(first, theirs, mine)
    flag[...] = jnp.zeros_like(flag)


PER = DK // ROWS


def plane_body(recv, _, send):
    total = jnp.sum(recv[...].astype(F32), axis=0).astype(BF16)
    for z in range(ZS):
        send[z, :, :SMALL] = total[:, :SMALL]
        send[z, :, SMALL:] = total[:, SMALL + z * QUART : SMALL + (z + 1) * QUART]


HALVES = WIDTH + MODEL // 2


def total_body(recv, keep, give):
    first = is_first()
    parts = [recv[z].astype(F32) for z in range(ZS)]
    even, odd = sum(parts[0::2]), sum(parts[1::2])
    small = jnp.concatenate(
        [even[:, :QUART], odd[:, :QUART], even[:, QUART:SMALL], odd[:, QUART:SMALL]], axis=1
    )
    rows = jnp.concatenate([even[:, SMALL:], odd[:, SMALL:]], axis=1)
    keep[:, :HALVES] = small
    give[:, :HALVES] = small
    pad = jnp.zeros((8, WIDTH), F32)
    keep[:, HALVES:] = jnp.concatenate([pick(first, rows[:8], rows[8:]), pad], axis=0)
    give[:, HALVES:] = jnp.concatenate([pick(first, rows[8:], rows[:8]), pad], axis=0)


def out_body(mine, theirs, down_o, up_o, w_o):
    first = is_first()
    halves = (pick(first, mine[...], theirs[...]), pick(first, theirs[...], mine[...]))
    wide = MODEL // 2
    for i, a in enumerate(halves):
        up_o[:, i * WIDTH : (i + 1) * WIDTH] = a[:, :WIDTH]
        down_o[:, i * wide : (i + 1) * wide] = a[:, WIDTH:HALVES]
        w_o[:, i * WIDTH : (i + 1) * WIDTH] = a[:8, HALVES:]


def swap(a):
    return lax.ppermute(a, "c", SWAP)


def cross(a):
    pairs = [(z * 2 + c, (z ^ 1) * 2 + (1 - c)) for z in range(ZS) for c in range(2)]
    return lax.ppermute(a, ("z", "c"), pairs)


def across(a):
    return lax.ppermute(a, "z", [(i, i ^ 1) for i in range(ZS)])


def a2a(a, axis):
    return lax.all_to_all(a, axis, 0, 0)


def local(inputs, queries, values, out_grad, key_weight, gate_down, gate_up, gate_bias):
    own = inputs[0]
    w_z = key_weight.reshape(1, 8, 2, 2, QUART).transpose(0, 3, 2, 1, 4)
    w_z = jnp.broadcast_to(w_z, (ZS // 2, 2, 2, 8, QUART))
    w_z = a2a(w_z.reshape(2 * ZS, 8, QUART), ("z", "c")).reshape(ZS * 16, QUART)
    w_all = a2a(jnp.broadcast_to(w_z[None], (PS, ZS * 16, QUART)), XY)

    third = shape((3 * TOK, QUART), BF16)
    mine, to_c, to_z, to_cz = kernel(prep_body, (third,) * 4, "prep", BIG)(
        queries[0], out_grad[0], values[0]
    )
    far = across(own)
    quad_bf = shape((QUAD, QUART), BF16)
    quad_f = shape((QUAD, QUART))
    tok, lat, logit, beta = kernel(
        gates_body,
        (shape((QUAD, MODEL), BF16), shape((QUAD, RANK), BF16), quad_f, quad_f), "gates", BIG,
    )(own, swap(own), far, swap(far), gate_down, gate_up, gate_bias[None])
    parts = (mine, swap(to_c), across(to_z), cross(to_cz))
    keys, send, w_all = kernel(
        keys_body,
        (quad_bf, shape((PS, 2 * ROWS + 16, DK), BF16), shape((PS, ZS * 16, QUART), BF16)),
        "keys", BIG, specs=[HBM] * 7, out_specs=(VM, VM, HBM), alias={0: 2},
        scratch=[pltpu.VMEM((PS, ZS * 16, QUART), BF16), pltpu.VMEM((QUAD, MODEL), BF16),
                 pltpu.VMEM((QUAD, QUART), F32), pltpu.VMEM((4, 3 * TOK, QUART), BF16)]
        + [pltpu.VMEM((QUAD, QUART), BF16)] * 3
        + [pltpu.VMEM((MODEL, QUART), BF16), pltpu.SemaphoreType.DMA((7,))],
    )(w_all, tok, beta, *parts)
    w_far = across(w_all)
    recv = a2a(send, XY)
    kd_local, local_part, q, g, v, add_g = kernel(
        inner_body, (quad_f, quad_f, quad_bf, quad_bf, quad_bf, shape((BLOCKS, WIDTH, DK))),
        "inner", BIG,
    )(*parts, keys, beta)
    recv = a2a(kernel(scan_body, shape((PS, 2 * ROWS, DK), BF16), "scan", 8)(recv), XY)
    kd, gate, up_part, lat_part = kernel(
        gate_body,
        (quad_bf, quad_bf, shape((RANK, QUART)), shape((RANK, QUAD))),
        "gate", BIG, specs=[VM] * 12 + [HBM], out_specs=(VM,) * 4,
        scratch=[pltpu.VMEM((QUAD, QUART), F32)],
    )(recv, add_g, keys, v, beta, q, g, kd_local, local_part, logit, lat, gate_up, w_far)
    lat_own, send = kernel(
        weight_body, (shape((RANK, TOK), BF16), shape((PS, 16, SMALL + ZS * QUART), BF16)),
        "weights", BIG,
    )(lat_part, swap(lat_part), across(lat_part), cross(lat_part), up_part, tok, kd)
    keep, give = kernel(
        through_body, (shape((TOK, MODEL)), shape((TOK, MODEL))), "through", BIG,
        scratch=[pltpu.VMEM((MODEL, QUART), BF16)] * 2,
    )(kd[:PAIR], across(kd[PAIR:]), w_all, w_far)
    piece = shape((TOK, QUART), BF16)
    gate_m, gate_c, gate_z, gate_cz = kernel(share_body, (piece,) * 4, "share", 8)(gate)
    input_grad, gate_grad, flag = kernel(
        input_body, (shape((TOK, MODEL), BF16), shape((TOK, 2 * WIDTH), BF16), shape((8, DK))),
        "input", 16,
    )(keep, swap(give), lat_own, gate_down, gate_m, swap(gate_c), across(gate_z), cross(gate_cz))
    send = kernel(plane_body, shape((ZS, 16, SMALL + QUART), BF16), "plane", 8)(
        a2a(send, XY), flag
    )
    end = shape((16, HALVES + WIDTH))
    keep, give = kernel(total_body, (end, end), "total", 8)(a2a(send, "z"))
    down_grad, up_grad, key_weight_grad = kernel(
        out_body,
        (shape((RANK, MODEL)), shape((RANK, 2 * WIDTH)), shape((8, 2 * WIDTH))), "grads", 8,
    )(keep, swap(give))
    return (input_grad[None], gate_grad[None], key_weight_grad, down_grad, up_grad)


def solution(mesh):
    grid = Mesh(mesh.devices.reshape(8, 4, 4, 2), ("z", "x", "y", "c"))
    seq = ("x", "y", "c")
    tok = P("z", seq, None)
    row = P(("z",) + seq, None)
    return jax.shard_map(
        local,
        mesh=grid,
        in_specs=(tok, tok, tok, tok, row, P(), P(), P()),
        out_specs=(tok, tok, row, P(), P()),
        check_vma=False,
    )
```

```python
import jax
import jax.numpy as jnp
from jax import lax
from jax.experimental import pallas as pl
from jax.experimental.pallas import tpu as pltpu
from jax.sharding import Mesh, PartitionSpec as P

HEADS = 8
DK = 128
GROUP = 64
HALF = HEADS // 2
WIDTH = HALF * DK
QUART = WIDTH // 2
PER_SEQ = QUART // DK
TOK = 128
PAIR = 2 * TOK
QUAD = 2 * PAIR
BLOCKS = PAIR // GROUP
MODEL = 2048
WIDE = MODEL // 4
RANK = 16
ZS = 8
PS = 16
ROWS = HALF * DK // PS
F32 = jnp.float32
BF16 = jnp.bfloat16
XY = ("x", "y")
SWAP = ((0, 1), (1, 0))
MB = 1 << 20


def shape(dims, dtype=F32):
    return jax.ShapeDtypeStruct(dims, dtype)


BIG = 56


VM = pl.BlockSpec(memory_space=pltpu.VMEM)
HBM = pl.BlockSpec(memory_space=pltpu.HBM)


def kernel(body, outs, name, limit, scratch=(), specs=None, out_specs=None, alias=None):
    extra = {} if specs is None else {"in_specs": specs, "out_specs": out_specs}
    if alias:
        extra["input_output_aliases"] = alias
    return pl.pallas_call(
        body,
        out_shape=outs,
        name=name,
        scratch_shapes=scratch,
        compiler_params=pltpu.CompilerParams(vmem_limit_bytes=limit * MB),
        **extra,
    )


def split(a):
    hi = a.astype(BF16)
    return hi, (a - hi.astype(F32)).astype(BF16)


def dot(a, b, dims=((1,), (0,))):
    return lax.dot_general(a, b, (dims, ((), ())), preferred_element_type=F32)


NT = ((1,), (1,))
TN = ((0,), (0,))


def dot_hl(a, b, dims=((1,), (0,))):
    hi, lo = split(b)
    return dot(a, hi, dims) + dot(a, lo, dims)


def dot_ff(a, b, dims=((1,), (0,))):
    ah, al = split(a)
    bh, bl = split(b)
    return dot(ah, bh, dims) + dot(ah, bl, dims) + dot(al, bh, dims)


def dot_mask(mask, b):
    hi, lo = split(b)
    rest = (b - hi.astype(F32) - lo.astype(F32)).astype(BF16)
    return dot(mask, hi) + dot(mask, lo) + dot(mask, rest)


def is_first():
    return lax.axis_index("c") == 0


def pick(first, a, b):
    return jnp.where(first, a, b)


def low_mask():
    rows = lax.broadcasted_iota(jnp.int32, (GROUP, GROUP), 0)
    cols = lax.broadcasted_iota(jnp.int32, (GROUP, GROUP), 1)
    return rows >= cols, rows <= cols


def tok_of(n):
    return slice(n * GROUP, (n + 1) * GROUP)


def col_of(h):
    return slice(h * DK, (h + 1) * DK)


def span_of(beta, n):
    return beta[(n + 1) * GROUP - 1 : (n + 1) * GROUP]


def odd_z():
    return lax.rem(lax.axis_index("z"), 2) == 1


def quarter_of(ref, core, odd):
    lo = pick(odd, ref[:, QUART : 2 * QUART], ref[:, :QUART])
    hi = pick(odd, ref[:, 3 * QUART :], ref[:, 2 * QUART : 3 * QUART])
    return pick(core, lo, hi)


def prep_body(q, g, v, keep, to_c, to_z, to_cz):
    first, odd = is_first(), odd_z()
    other, even = jnp.logical_not(first), jnp.logical_not(odd)
    for i, ref in enumerate((q, g, v)):
        rows = slice(i * TOK, (i + 1) * TOK)
        keep[rows] = quarter_of(ref, first, odd)
        to_c[rows] = quarter_of(ref, other, odd)
        to_z[rows] = quarter_of(ref, first, even)
        to_cz[rows] = quarter_of(ref, other, even)


def rows_of(seq, n):
    at = seq * PAIR + n * GROUP
    return slice(at, at + GROUP)


def state_of(seq, h):
    return seq * PER_SEQ + h


def gates_body(own, peer, far, far_peer, down, up, bias, tok, lat, logit, beta):
    first, odd = is_first(), odd_z()
    tok[:TOK] = pick(first, own[...], peer[...])
    tok[TOK:PAIR] = pick(first, peer[...], own[...])
    tok[PAIR : PAIR + TOK] = pick(first, far[...], far_peer[...])
    tok[PAIR + TOK :] = pick(first, far_peer[...], far[...])
    latent = dot(tok[...], down[...], NT).astype(BF16)
    lat[...] = latent
    x = dot(latent, quarter_of(up, first, odd)) + quarter_of(bias, first, odd)
    logit[...] = x
    gamma = (jnp.minimum(x, 0.0) - jnp.log1p(jnp.exp(-jnp.abs(x)))) * (1.0 / 16.0)
    lower = low_mask()[0].astype(BF16)
    for n in range(QUAD // GROUP):
        beta[tok_of(n)] = dot_mask(lower, gamma[tok_of(n)])


def assemble(out, a, b, c, d):
    first = is_first()
    out[:TOK] = pick(first, a, b)
    out[TOK:PAIR] = pick(first, b, a)
    out[PAIR : PAIR + TOK] = pick(first, c, d)
    out[PAIR + TOK :] = pick(first, d, c)


def added_grads(q, g, beta, seq, n):
    r = rows_of(seq, n)
    b = beta[r]
    scaled = q[r].astype(F32) * jnp.exp(b)
    grad = g[r]
    return [dot_hl(grad[:, col_of(h)], scaled[:, col_of(h)], TN) for h in range(PER_SEQ)], b[-1:]


def start_states(q, g, beta, send):
    run = [jnp.zeros((DK, DK), F32)] * HALF
    decays = []
    for seq in range(2):
        total = jnp.zeros((1, QUART), F32)
        for n in reversed(range(BLOCKS)):
            parts, last = added_grads(q, g, beta, seq, n)
            total = total + last
            decay = jnp.exp(last)
            for h in range(PER_SEQ):
                s = state_of(seq, h)
                run[s] = decay[:, col_of(h)] * run[s] + parts[h]
        decays.append(jnp.exp(total))
    for p in range(PS):
        s, at = p // PER, (p % PER) * ROWS
        row = decays[s // PER_SEQ][:, col_of(s % PER_SEQ)]
        send[p, :ROWS] = run[s][at : at + ROWS].astype(BF16)
        top = row.astype(BF16).astype(F32)
        send[p, ROWS : ROWS + 16] = jnp.concatenate(
            [jnp.broadcast_to(top, (8, DK)), jnp.broadcast_to(row - top, (8, DK))], axis=0
        ).astype(BF16)


def added_states(key, v, beta, seq, n):
    r = rows_of(seq, n)
    b = beta[r]
    last = b[GROUP - 1 : GROUP]
    tail = key[r].astype(F32) * jnp.exp(last - b)
    vals = v[r]
    return [dot_hl(vals[:, col_of(h)], tail[:, col_of(h)], TN) for h in range(PER_SEQ)], jnp.exp(last)


def load(pairs, sems):
    copies = [pltpu.make_async_copy(a, b, sems.at[i]) for i, (a, b) in enumerate(pairs)]
    for copy in copies:
        copy.start()
    return copies


def unpack(recv, w):
    for p in range(PS):
        for z in range(ZS):
            w[z * 256 + p * 16 : z * 256 + p * 16 + 16] = recv[p, z * 16 : z * 16 + 16]


def keys_body(recv_h, tok_h, beta_h, mine, from_c, from_z, from_cz, key_o, send, w_o,
              recv, tok, beta, parts, q, g, v, w, sems):
    copies = load(
        [(beta_h, beta)]
        + [(a, parts.at[i]) for i, a in enumerate((mine, from_c, from_z, from_cz))]
        + [(recv_h, recv), (tok_h, tok)],
        sems,
    )
    for copy in copies[:5]:
        copy.wait()
    for i, out in enumerate((q, g, v)):
        assemble(out, *(parts[j, i * TOK : (i + 1) * TOK] for j in range(4)))
    start_states(q, g, beta, send)
    copies[5].wait()
    unpack(recv, w)
    copies[6].wait()
    key_o[...] = dot(tok[...], w[...]).astype(BF16)
    run = [jnp.zeros((DK, DK), F32)] * HALF
    for seq in range(2):
        for n in range(BLOCKS):
            parts, decay = added_states(key_o, v, beta, seq, n)
            for h in range(PER_SEQ):
                s = state_of(seq, h)
                run[s] = decay[:, col_of(h)] * run[s] + parts[h]
    for p in range(PS):
        s, at = p // PER, (p % PER) * ROWS
        send[p, ROWS + 16 :] = run[s][at : at + ROWS].astype(BF16)


def scan_body(recv, send):
    def decay(p):
        rows = recv[p, ROWS : ROWS + 16].astype(F32)
        return rows[:1] + rows[8:9]

    run = jnp.zeros((ROWS, DK), F32)
    for p in reversed(range(PS)):
        send[p, :ROWS] = run.astype(BF16)
        run = decay(p) * run + recv[p, :ROWS].astype(F32)
    run = jnp.zeros((ROWS, DK), F32)
    for p in range(PS):
        send[p, ROWS:] = run.astype(BF16)
        run = decay(p) * run + recv[p, ROWS + 16 :].astype(F32)


def inner_body(mine, from_c, from_z, from_cz, key_r, beta, logit,
               kd_o, local, q_r, g_r, v_r, adds, slope):
    slope[...] = 1.0 / (1.0 + jnp.exp(logit[...])) * (1.0 / 16.0)
    low, high = low_mask()
    for i, out in enumerate((q_r, g_r, v_r)):
        rows = slice(i * TOK, (i + 1) * TOK)
        assemble(out, mine[rows], from_c[rows], from_z[rows], from_cz[rows])
    for seq in range(2):
        for n in range(BLOCKS):
            parts, _ = added_grads(q_r, g_r, beta, seq, n)
            for h in range(PER_SEQ):
                adds[n, col_of(state_of(seq, h))] = parts[h]
    for n in range(QUAD // GROUP):
        r = tok_of(n)
        b = beta[r]
        grow, shrink = jnp.exp(b), jnp.exp(-b)
        q = q_r[r].astype(F32)
        k = key_r[r].astype(F32)
        q_s, k_s = q * grow, k * shrink
        for h in range(PER_SEQ):
            c = col_of(h)
            g, v = g_r[r, c], v_r[r, c]
            pairs = jnp.where(low, dot(g, v, NT), 0.0)
            pairs_t = jnp.where(high, dot(v, g, NT), 0.0)
            kd = shrink[:, c] * dot_ff(pairs_t, q_s[:, c])
            qd = grow[:, c] * dot_ff(pairs, k_s[:, c])
            kd_o[r, c] = kd
            local[r, c] = q[:, c] * qd - k[:, c] * kd


def chip_rows(recv, at):
    return [
        jnp.concatenate([recv[s * PER + i, at : at + ROWS] for i in range(PER)], axis=0).astype(F32)
        for s in range(HALF)
    ]


def gate_body(recv, adds, key_r, v_r, beta, q_r, g_r, kd_in, local, slope, lat, up, _,
              kd_o, gate_o, up_part, lat_part, delta):
    first, odd = is_first(), odd_z()
    high = low_mask()[1].astype(BF16)
    back, run = chip_rows(recv, 0), chip_rows(recv, ROWS)
    grads = list(back)
    for seq in range(2):
        states = [state_of(seq, h) for h in range(PER_SEQ)]
        for n in reversed(range(BLOCKS)):
            r = rows_of(seq, n)
            b = beta[r]
            last = b[GROUP - 1 : GROUP]
            decay = jnp.exp(last)
            kd = jnp.concatenate(
                [dot_hl(v_r[r, col_of(h)], grads[s]) for h, s in enumerate(states)], axis=1
            ) * jnp.exp(last - b)
            kd_o[r] = (kd + kd_in[r]).astype(BF16)
            delta[r] = local[r] - key_r[r].astype(F32) * kd
            for h, s in enumerate(states):
                grads[s] = decay[:, col_of(h)] * grads[s] + adds[n, col_of(s)]
        for n in range(BLOCKS):
            r = rows_of(seq, n)
            parts, decay = added_states(key_r, v_r, beta, seq, n)
            qd = jnp.concatenate(
                [dot_hl(g_r[r, col_of(h)], run[s]) for h, s in enumerate(states)], axis=1
            ) * jnp.exp(beta[r])
            delta[r] += q_r[r].astype(F32) * qd
            for h, s in enumerate(states):
                run[s] = decay[:, col_of(h)] * run[s] + parts[h]
        beyond = jnp.concatenate(
            [jnp.sum(run[s] * back[s], axis=0, keepdims=True) for s in states], axis=1
        )
        for n in reversed(range(BLOCKS)):
            r = rows_of(seq, n)
            suffix = dot_mask(high, delta[r]) + beyond
            beyond = suffix[:1]
            gate_o[r] = (suffix * slope[r]).astype(BF16)
    gate = gate_o[...]
    up_part[...] = dot(lat[...], gate, TN)
    lat_part[...] = dot(quarter_of(up, first, odd), gate, NT)


SMALL = QUART + WIDE


def weight_body(lat_a, lat_c, lat_z, lat_cz, up_part, tok, kd_r, lat_o, send):
    first, odd = is_first(), odd_z()
    near = lat_a[...] + lat_c[...]
    far = lat_z[...] + lat_cz[...]
    latent = jnp.concatenate(
        [near[:, :PAIR] + far[:, PAIR:], near[:, PAIR:] + far[:, :PAIR]], axis=1
    ).astype(BF16)
    lat_o[...] = pick(first, latent[:, :TOK], latent[:, TOK:PAIR])
    lo = pick(odd, tok[:, WIDE : 2 * WIDE], tok[:, :WIDE])
    hi = pick(odd, tok[:, 3 * WIDE :], tok[:, 2 * WIDE : 3 * WIDE])
    down = dot(latent, pick(first, lo, hi))
    small = jnp.concatenate([up_part[...], down], axis=1).astype(BF16)
    for p in range(PS):
        send[p, :, :SMALL] = small
    kd = kd_r[...]
    for z in range(ZS):
        block = dot(tok[:, z * 256 : z * 256 + 256], kd, TN).astype(BF16)
        lanes = slice(SMALL + z * QUART, SMALL + (z + 1) * QUART)
        for p in range(PS):
            send[p, :, lanes] = block[p * 16 : p * 16 + 16]


def share_body(gate, keep, to_c, to_z, to_cz):
    first = is_first()
    keep[...] = pick(first, gate[:TOK], gate[TOK:PAIR])
    to_c[...] = pick(first, gate[TOK:PAIR], gate[:TOK])
    to_z[...] = pick(first, gate[PAIR : PAIR + TOK], gate[PAIR + TOK :])
    to_cz[...] = pick(first, gate[PAIR + TOK :], gate[PAIR : PAIR + TOK])


def through_body(kd, kd_far, w_all, far_all, keep, give, w, w_far):
    first = is_first()
    unpack(w_all, w)
    unpack(far_all, w_far)
    total = dot(kd[...], w[...], NT) + dot(kd_far[...], w_far[...], NT)
    give[...] = pick(first, total[TOK:], total[:TOK])
    keep[...] = pick(first, total[:TOK], total[TOK:])


def input_body(keep, got, lat, down, gate_m, gate_c, gate_z, gate_cz, out, gate, flag):
    first, odd = is_first(), odd_z()
    out[...] = (keep[...] + got[...] + dot(lat[...], down[...], TN)).astype(BF16)
    mine = jnp.concatenate(
        [pick(odd, gate_z[...], gate_m[...]), pick(odd, gate_m[...], gate_z[...])], axis=1
    )
    theirs = jnp.concatenate(
        [pick(odd, gate_cz[...], gate_c[...]), pick(odd, gate_c[...], gate_cz[...])], axis=1
    )
    gate[:, :WIDTH] = pick(first, mine, theirs)
    gate[:, WIDTH:] = pick(first, theirs, mine)
    flag[...] = jnp.zeros_like(flag)


PER = DK // ROWS


def plane_body(recv, _, send):
    total = jnp.sum(recv[...].astype(F32), axis=0).astype(BF16)
    for z in range(ZS):
        send[z, :, :SMALL] = total[:, :SMALL]
        send[z, :, SMALL:] = total[:, SMALL + z * QUART : SMALL + (z + 1) * QUART]


HALVES = WIDTH + MODEL // 2


def total_body(recv, keep, give):
    first = is_first()
    parts = [recv[z].astype(F32) for z in range(ZS)]
    even, odd = sum(parts[0::2]), sum(parts[1::2])
    small = jnp.concatenate(
        [even[:, :QUART], odd[:, :QUART], even[:, QUART:SMALL], odd[:, QUART:SMALL]], axis=1
    )
    rows = jnp.concatenate([even[:, SMALL:], odd[:, SMALL:]], axis=1)
    keep[:, :HALVES] = small
    give[:, :HALVES] = small
    pad = jnp.zeros((8, WIDTH), F32)
    keep[:, HALVES:] = jnp.concatenate([pick(first, rows[:8], rows[8:]), pad], axis=0)
    give[:, HALVES:] = jnp.concatenate([pick(first, rows[8:], rows[:8]), pad], axis=0)


def out_body(mine, theirs, down_o, up_o, w_o):
    first = is_first()
    halves = (pick(first, mine[...], theirs[...]), pick(first, theirs[...], mine[...]))
    wide = MODEL // 2
    for i, a in enumerate(halves):
        up_o[:, i * WIDTH : (i + 1) * WIDTH] = a[:, :WIDTH]
        down_o[:, i * wide : (i + 1) * wide] = a[:, WIDTH:HALVES]
        w_o[:, i * WIDTH : (i + 1) * WIDTH] = a[:8, HALVES:]


def swap(a):
    return lax.ppermute(a, "c", SWAP)


def cross(a):
    pairs = [(z * 2 + c, (z ^ 1) * 2 + (1 - c)) for z in range(ZS) for c in range(2)]
    return lax.ppermute(a, ("z", "c"), pairs)


def across(a):
    return lax.ppermute(a, "z", [(i, i ^ 1) for i in range(ZS)])


def a2a(a, axis):
    return lax.all_to_all(a, axis, 0, 0)


def local(inputs, queries, values, out_grad, key_weight, gate_down, gate_up, gate_bias):
    own = inputs[0]
    w_z = key_weight.reshape(1, 8, 2, 2, QUART).transpose(0, 3, 2, 1, 4)
    w_z = jnp.broadcast_to(w_z, (ZS // 2, 2, 2, 8, QUART))
    w_z = a2a(w_z.reshape(2 * ZS, 8, QUART), ("z", "c")).reshape(ZS * 16, QUART)
    w_all = a2a(jnp.broadcast_to(w_z[None], (PS, ZS * 16, QUART)), XY)

    third = shape((3 * TOK, QUART), BF16)
    mine, to_c, to_z, to_cz = kernel(prep_body, (third,) * 4, "prep", BIG)(
        queries[0], out_grad[0], values[0]
    )
    far = across(own)
    quad_bf = shape((QUAD, QUART), BF16)
    quad_f = shape((QUAD, QUART))
    tok, lat, logit, beta = kernel(
        gates_body,
        (shape((QUAD, MODEL), BF16), shape((QUAD, RANK), BF16), quad_f, quad_f), "gates", BIG,
    )(own, swap(own), far, swap(far), gate_down, gate_up, gate_bias[None])
    parts = (mine, swap(to_c), across(to_z), cross(to_cz))
    keys, send, w_all = kernel(
        keys_body,
        (quad_bf, shape((PS, 2 * ROWS + 16, DK), BF16), shape((PS, ZS * 16, QUART), BF16)),
        "keys", BIG, specs=[HBM] * 7, out_specs=(VM, VM, HBM), alias={0: 2},
        scratch=[pltpu.VMEM((PS, ZS * 16, QUART), BF16), pltpu.VMEM((QUAD, MODEL), BF16),
                 pltpu.VMEM((QUAD, QUART), F32), pltpu.VMEM((4, 3 * TOK, QUART), BF16)]
        + [pltpu.VMEM((QUAD, QUART), BF16)] * 3
        + [pltpu.VMEM((MODEL, QUART), BF16), pltpu.SemaphoreType.DMA((7,))],
    )(w_all, tok, beta, *parts)
    w_far = across(w_all)
    recv = a2a(send, XY)
    kd_local, local_part, q, g, v, add_g, slope = kernel(
        inner_body, (quad_f, quad_f, quad_bf, quad_bf, quad_bf, shape((BLOCKS, WIDTH, DK)), quad_f),
        "inner", BIG,
    )(*parts, keys, beta, logit)
    recv = a2a(kernel(scan_body, shape((PS, 2 * ROWS, DK), BF16), "scan", 8)(recv), XY)
    kd, gate, up_part, lat_part = kernel(
        gate_body,
        (quad_bf, quad_bf, shape((RANK, QUART)), shape((RANK, QUAD))),
        "gate", BIG, specs=[VM] * 12 + [HBM], out_specs=(VM,) * 4,
        scratch=[pltpu.VMEM((QUAD, QUART), F32)],
    )(recv, add_g, keys, v, beta, q, g, kd_local, local_part, slope, lat, gate_up, w_far)
    lat_own, send = kernel(
        weight_body, (shape((RANK, TOK), BF16), shape((PS, 16, SMALL + ZS * QUART), BF16)),
        "weights", BIG,
    )(lat_part, swap(lat_part), across(lat_part), cross(lat_part), up_part, tok, kd)
    keep, give = kernel(
        through_body, (shape((TOK, MODEL)), shape((TOK, MODEL))), "through", BIG,
        scratch=[pltpu.VMEM((MODEL, QUART), BF16)] * 2,
    )(kd[:PAIR], across(kd[PAIR:]), w_all, w_far)
    piece = shape((TOK, QUART), BF16)
    gate_m, gate_c, gate_z, gate_cz = kernel(share_body, (piece,) * 4, "share", 8)(gate)
    input_grad, gate_grad, flag = kernel(
        input_body, (shape((TOK, MODEL), BF16), shape((TOK, 2 * WIDTH), BF16), shape((8, DK))),
        "input", 16,
    )(keep, swap(give), lat_own, gate_down, gate_m, swap(gate_c), across(gate_z), cross(gate_cz))
    send = kernel(plane_body, shape((ZS, 16, SMALL + QUART), BF16), "plane", 8)(
        a2a(send, XY), flag
    )
    end = shape((16, HALVES + WIDTH))
    keep, give = kernel(total_body, (end, end), "total", 8)(a2a(send, "z"))
    down_grad, up_grad, key_weight_grad = kernel(
        out_body,
        (shape((RANK, MODEL)), shape((RANK, 2 * WIDTH)), shape((8, 2 * WIDTH))), "grads", 8,
    )(keep, swap(give))
    return (input_grad[None], gate_grad[None], key_weight_grad, down_grad, up_grad)


def solution(mesh):
    grid = Mesh(mesh.devices.reshape(8, 4, 4, 2), ("z", "x", "y", "c"))
    seq = ("x", "y", "c")
    tok = P("z", seq, None)
    row = P(("z",) + seq, None)
    return jax.shard_map(
        local,
        mesh=grid,
        in_specs=(tok, tok, tok, tok, row, P(), P(), P()),
        out_specs=(tok, tok, row, P(), P()),
        check_vma=False,
    )
```
